256 devices in a mesh: pb: 64 (over z, x, core), ka: 4 (over y).
Axes of the slice: x: 4, y: 4, z: 8, core: 2. Of those that a mesh axis runs over, the one named last changes fastest.
Arguments:
- queries: bfloat16 [65536, 512], P('pb'), may hold values from -80 to 80
- key_cache: bfloat16 [65536, 128], P(('ka', 'pb')), may hold values from -4.1 to 4.1
- value_cache: bfloat16 [65536, 128], P(('ka', 'pb')), may hold values from -4 to 4
- block_list: int32 [512, 32], P('pb'), may hold values from 0 to 511, as said below
- block_count: int32 [512], P('pb'), may hold values from 1 to 32, as said below
Outputs:
- attended: bfloat16 [65536, 512], P(('pb', 'ka'))
The draws below stay inside these ranges and needn't reach their ends.
Inputs may be any that keep to these rules, and one draw needn't show every extreme that they name: `block_list`: entries of row qb before block_count[qb] are distinct blocks at most qb, and qb itself is among them. They are the blocks v at most qb of one set of 16 vertical blocks, then the blocks qb - o at least 0 (and not already listed) of one set of 16 slash offsets; both sets contain 0 and lie below 128. Later entries equal qb. `block_count`: the number of distinct listed blocks of each query block.
All inputs are finite; a program needn't handle non-finite values.
Results may differ from the reference program's by a relative error of at most 0.0046.
Values may be sent and summed in bfloat16 or wider, within the bound.
A program may use at most 128 MiB of HBM per device.

```python
import math
import jax
import jax.numpy as jnp
from jax import lax

HD = 128
QH = 4
BLK = 128
LIST = 32
NV = 16
NQB = 512
SEQ = 65536
N_KA = 4


def build_lists(key):
    vertical_key, offset_key = jax.random.split(jax.random.fold_in(key, 11))
    quarter = NQB // 4
    verticals = jnp.concatenate([jnp.zeros((1,), jnp.int32), 1 + jax.random.permutation(vertical_key, quarter - 1)[:NV - 1].astype(jnp.int32)])
    offsets = jnp.concatenate([jnp.zeros((1,), jnp.int32), 1 + jax.random.permutation(offset_key, quarter - 1)[:LIST - NV - 1].astype(jnp.int32)])
    block_ids = jnp.arange(NQB, dtype=jnp.int32)[:, None]
    vertical_ok = verticals[None, :] <= block_ids
    slash_blocks = block_ids - offsets[None, :]
    repeated = jnp.any((slash_blocks[:, :, None] == verticals[None, None, :]) & vertical_ok[:, None, :], axis=2)
    slash_ok = (slash_blocks >= 0) & jnp.logical_not(repeated)
    candidate = jnp.concatenate([jnp.broadcast_to(verticals[None, :], (NQB, NV)), slash_blocks], axis=1)
    usable = jnp.concatenate([vertical_ok, slash_ok], axis=1)
    slot_ids = jnp.arange(LIST, dtype=jnp.int32)[None, :]
    ordering = jnp.argsort(jnp.where(usable, slot_ids, LIST + slot_ids), axis=1)
    arranged = jnp.take_along_axis(candidate, ordering, axis=1)
    live_count = jnp.sum(usable.astype(jnp.int32), axis=1)
    listed = jnp.where(slot_ids < live_count[:, None], arranged, block_ids)
    return (listed.astype(jnp.int32), live_count.astype(jnp.int32))


def draw_block_list(key, part):
    return build_lists(key)[0]


def draw_block_count(key, part):
    return build_lists(key)[1]


def draw_base(key):
    return jnp.clip(jax.random.normal(jax.random.fold_in(key, 21), (SEQ, HD), jnp.float32), -4.0, 4.0)


def draw_key_cache(key, part):
    base_keys = draw_base(key)
    return base_keys.astype(jnp.bfloat16)


def draw_queries(key, part):
    values = jnp.clip(jax.random.normal(jax.random.fold_in(key, 22), (SEQ, QH * HD), jnp.float32), -4.0, 4.0)
    return values.astype(jnp.bfloat16)


def steps_of(rng, shape, shards, low, largest):
    level, own = 1.0, jax.random.fold_in(rng, 6)
    for dim, parts in shards:
        draws = jnp.exp(jax.random.uniform(jax.random.fold_in(own, dim), (parts,), jnp.float32, low / len(shards), largest / len(shards)))
        level = level * jnp.repeat(draws, shape[dim] // parts).reshape([-1 if axis == dim else 1 for axis in range(len(shape))])
    return level


def normal_values(rng, dims, spread, most, shards=(), kind=jnp.bfloat16):
    values = jax.random.normal(rng, dims, jnp.float32) * spread
    if len(shards) > 0:
        values = steps_of(rng, dims, shards, -0.22, 0.18) * values
    return jnp.clip(values, min=-most, max=most).astype(kind)


def setup_inputs(seed: int = 0) -> dict:
    keys = jax.random.split(jax.random.key(seed), 6)
    queries = draw_queries(jax.random.fold_in(keys[5], 71), 0)
    key_cache = draw_key_cache(jax.random.fold_in(keys[5], 71), 0)
    value_cache = normal_values(keys[2], (SEQ, HD), 1.0, 4.0, ((0, 256),))
    block_list = draw_block_list(jax.random.fold_in(keys[5], 71), 0)
    block_count = draw_block_count(jax.random.fold_in(keys[5], 71), 0)
    return {"queries": queries, "key_cache": key_cache, "value_cache": value_cache, "block_list": block_list, "block_count": block_count}


masked_score = -1e+30

def reference(queries, key_cache, value_cache, block_list, block_count):
    score_scale = 1.0 / math.sqrt(HD)
    total_blocks = block_list.shape[0]
    shard_width = total_blocks // N_KA
    key_blocks = key_cache.reshape(total_blocks, BLK, HD)
    value_blocks = value_cache.reshape(total_blocks, BLK, HD)
    slot_ids = jnp.arange(LIST, dtype=jnp.int32)
    shard_ids = jnp.arange(N_KA, dtype=jnp.int32)
    position = jnp.arange(BLK, dtype=jnp.int32)

    def one_block(block_pos):
        query_rows = lax.dynamic_slice_in_dim(queries, block_pos * BLK, BLK, 0)
        query_rows = query_rows.reshape(BLK, QH, HD).astype(jnp.float32)
        listed = block_list[block_pos]
        live_count = block_count[block_pos]
        key_tiles = key_blocks[listed].astype(jnp.float32)
        value_tiles = value_blocks[listed].astype(jnp.float32)
        scores = jnp.einsum('qhd,skd->hqsk', query_rows, key_tiles) * score_scale
        earlier = (listed < block_pos)[None, :, None]
        diagonal = (listed == block_pos)[None, :, None] & (position[None, None, :] <= position[:, None, None])
        valid = (slot_ids < live_count)[None, :, None] & (earlier | diagonal)
        masked = jnp.where(valid[None], scores, masked_score)
        slot_peak = lax.optimization_barrier(jnp.max(masked, axis=3))
        shard_of = (listed // shard_width).astype(jnp.int32)
        in_shard = shard_of[:, None] == shard_ids[None, :]
        shard_peak = lax.optimization_barrier(jnp.max(jnp.where(in_shard[None, None], slot_peak[..., None], masked_score), axis=2))
        peak_slot = jnp.take(shard_peak, shard_of, axis=2)
        weights = jnp.where(valid[None], jnp.exp(scores - peak_slot[..., None]), 0.0)
        membership = in_shard.astype(jnp.float32)
        shard_sum = jnp.einsum('hqs,sj->hqj', lax.optimization_barrier(jnp.sum(weights, axis=3)), membership)
        rounded = lax.optimization_barrier(weights.astype(jnp.bfloat16)).astype(jnp.float32)
        per_slot = jnp.einsum('hqsk,skd->hqsd', rounded, value_tiles)
        shard_out = jnp.einsum('hqsd,sj->hqjd', per_slot, membership)
        overall = lax.optimization_barrier(jnp.max(shard_peak, axis=2))
        factor = jnp.exp(shard_peak - overall[..., None])
        numerator = jnp.einsum('hqjd,hqj->hqd', shard_out, factor)
        denominator = lax.optimization_barrier(jnp.sum(shard_sum * factor, axis=2))
        result = numerator / denominator[..., None]
        return jnp.transpose(result, (1, 0, 2)).reshape(BLK, QH * HD).astype(jnp.bfloat16)
    blocks_out = lax.map(one_block, jnp.arange(total_blocks, dtype=jnp.int32))
    return blocks_out.reshape(total_blocks * BLK, QH * HD)
```

```python
import functools
import math

import jax
import jax.numpy as jnp
from jax import lax
from jax.experimental import pallas as pl
from jax.experimental.pallas import tpu as pltpu
from jax.sharding import PartitionSpec as P

HD = 128
QH = 4
BLK = 128
LIST = 32
NV = 16
PART = 16
CHUNK = 4
MASKED = -1e30
FACTOR = math.log2(math.e) / math.sqrt(HD)


def attention_kernel(
    list_ref, count_ref, q_hbm, k_hbm, v_hbm, out_ref,
    buf, vbuf, qs, kc, vc, s_ref, acc_ref, m_ref, l_ref,
    q_sem, z_send, z_recv, p1_send, p1_recv, p2_send, p2_recv, sib_send, sib_recv,
    vz_send, vz_recv, vx_send, vx_recv, vy_send, vy_recv, vs_send, vs_recv,
):
    p = lax.axis_index("pb")
    y = lax.axis_index("ka")
    z = p // 8
    x = (p // 2) % 4
    c = p % 2

    def dev(zz, xx, cc, yy):
        return (zz * 8 + xx * 2 + cc, yy)

    def remote(src, dst, ssem, rsem, device):
        return pltpu.make_async_remote_copy(
            src_ref=src, dst_ref=dst, send_sem=ssem, recv_sem=rsem,
            device_id=device, device_id_type=pl.DeviceIdType.MESH,
        )

    def have(hi):
        return z >= 2 - hi

    def needed(hi, g, xx):
        if hi == 1:
            return have(hi)
        if hi == 0:
            return have(hi) & ((g >= xx) | (z == 2))
        return g <= xx

    q_copy = pltpu.make_async_copy(q_hbm.at[pl.ds(pl.multiple_of(y * 256, 256), 256)], qs, q_sem)
    q_copy.start()

    src = (k_hbm, v_hbm)
    g_own = z % 4

    def z_target(kv):
        return (x, g_own) if kv == 0 else (g_own, x)

    def z_plane(d):
        return 2 * y + z // 4 + d

    def z_copy(kv, d):
        xd, yd = z_target(kv)
        region = buf.at[kv, 2 - d, g_own, x, c]
        return remote(src[kv], region, z_send.at[kv, d], z_recv.at[kv, 2 - d], dev(z_plane(d), xd, c, yd))

    def z_self(kv, d):
        xd, yd = z_target(kv)
        return (z_plane(d) == z) & (xd == x) & (yd == y)

    for d in range(3):
        for kv in range(2):
            live = z_plane(d) <= 7
            own = z_self(kv, d)

            @pl.when(live & jnp.logical_not(own))
            def _():
                z_copy(kv, d).start()

            @pl.when(live & own)
            def _():
                pltpu.make_async_copy(src[kv], buf.at[kv, 2 - d, g_own, x, c], z_recv.at[kv, 2 - d]).start()

    def row(kv):
        return y if kv == 0 else x

    def col(kv):
        return x if kv == 0 else y

    def along(kv, i):
        return dev(z, (x + i) % 4, c, y) if kv == 0 else dev(z, x, c, (y + i) % 4)

    def across(kv, i):
        return dev(z, x, c, (y + i) % 4) if kv == 0 else dev(z, (x + i) % 4, c, y)

    sibling = dev(z, x, 1 - c, y)

    def p1_copy(kv, hi, i):
        region = buf.at[kv, hi, row(kv), col(kv), c]
        return remote(region, region, p1_send.at[kv, hi, i - 1], p1_recv.at[kv, hi, i - 1], along(kv, i))

    def p1_live(kv, hi, i):
        return needed(hi, y, (x + i) % 4) if kv == 0 else have(hi)

    def p2_copy(kv, hi, i):
        region = buf.at[kv, hi, row(kv), :, c]
        return remote(region, region, p2_send.at[kv, hi, i - 1], p2_recv.at[kv, hi, i - 1], across(kv, i))

    def p2_live(kv, hi, i):
        return needed(hi, y, x) if kv == 0 else needed(hi, x, (x + i) % 4)

    def sib_copy(kv, hi, g):
        region = buf.at[kv, hi, g, :, c]
        return remote(region, region, sib_send.at[kv, hi, g], sib_recv.at[kv, hi, g], sibling)

    for hi in (1, 2, 0):
        for kv in range(2):

            @pl.when(have(hi))
            def _():
                pltpu.make_async_copy(src[kv], buf.at[kv, hi, row(kv), col(kv), c], z_recv.at[kv, hi]).wait()

            for i in (1, 3, 2):

                @pl.when(p1_live(kv, hi, i))
                def _():
                    p1_copy(kv, hi, i).start()

    for hi in (1, 2, 0):
        for kv in range(2):
            for i in (1, 3, 2):
                got = needed(hi, y, x) if kv == 0 else have(hi)

                @pl.when(got)
                def _():
                    region = buf.at[kv, hi, row(kv), (col(kv) + 4 - i) % 4, c]
                    remote(region, region, p1_send.at[kv, hi, i - 1], p1_recv.at[kv, hi, i - 1], sibling).wait_recv()

            for i in (1, 3, 2):

                @pl.when(p2_live(kv, hi, i))
                def _():
                    p2_copy(kv, hi, i).start()

            @pl.when(needed(hi, row(kv), x))
            def _():
                sib_copy(kv, hi, row(kv)).start()

    for hi in (1, 2, 0):
        for i in (1, 3, 2):
            for kv in range(2):
                g = (row(kv) + 4 - i) % 4

                @pl.when(needed(hi, g, x))
                def _():
                    region = buf.at[kv, hi, g, :, c]
                    remote(region, region, p2_send.at[kv, hi, i - 1], p2_recv.at[kv, hi, i - 1], sibling).wait_recv()
                    sib_copy(kv, hi, g).start()

    for hi in (1, 2, 0):
        for kv in range(2):
            for g in range(4):

                @pl.when(needed(hi, g, x))
                def _():
                    region = buf.at[kv, hi, g, :, 1 - c]
                    remote(region, region, sib_send.at[kv, hi, g], sib_recv.at[kv, hi, g], sibling).wait_recv()

    def vz_copy(i):
        return remote(vbuf.at[c, x, y], vbuf.at[c, x, y], vz_send.at[i], vz_recv, dev(3 + i, x, c, y))

    def vx_copy(i):
        return remote(
            vbuf.at[c, x, y], vbuf.at[c, x, y], vx_send.at[i - 1], vx_recv.at[i - 1], dev(z, (x + i) % 4, c, y)
        )

    def vy_copy(i):
        return remote(
            vbuf.at[c, :, y], vbuf.at[c, :, y], vy_send.at[i - 1], vy_recv.at[i - 1], dev(z, x, c, (y + i) % 4)
        )

    def vs_copy(cc):
        return remote(vbuf.at[cc], vbuf.at[cc], vs_send, vs_recv, sibling)

    def place(block):
        rel = jnp.clip(block - 64 * (z - 2), 0, 191)
        return rel >> 6, (rel >> 4) & 3, (rel >> 2) & 3, (rel >> 1) & 1, rel & 1

    def block_of(kv, block):
        hi, g, l, cc, r = place(block)
        return buf[kv, hi, g, l, cc, r]

    @pl.when(z == 2)
    def _():
        entries = [list_ref[2 * y, i] for i in range(NV)]
        chosen = jnp.int32(0)
        for i in range(NV):
            rank = jnp.int32(0)
            for j in range(NV):
                if j != i:
                    rank = rank + jnp.where(entries[j] < entries[i], 1, 0)
            chosen = chosen + jnp.where(rank == 4 * x + y, entries[i], 0)
        vbuf[c, x, y] = block_of(c, chosen)
        for i in (0, 4, 1, 3, 2):
            vz_copy(i).start()

    @pl.when(z >= 3)
    def _():
        vz_copy(0).wait_recv()
        for i in (1, 3, 2):
            vx_copy(i).start()

    delta = lax.broadcasted_iota(jnp.int32, (BLK, BLK), 1) - lax.broadcasted_iota(jnp.int32, (BLK, BLK), 0)

    def load_part(part):
        def load(n, _):
            q = n // PART
            s = n % PART
            block = list_ref[2 * y + q, part * PART + s]
            rows = pl.ds(pl.multiple_of(s * BLK, BLK), BLK)
            kc[q, rows, :] = block_of(0, block)
            vc[q, rows, :] = block_of(1, block)
            return 0

        lax.fori_loop(0, 2 * PART, load, 0)

    def attend(q, part):
        my_block = 8 * p + 2 * y + q
        count = count_ref[2 * y + q]
        rows = pl.ds(pl.multiple_of(q * BLK, BLK), BLK)
        q4 = jnp.concatenate([qs[rows, h * HD : (h + 1) * HD] for h in range(QH)], axis=0)
        width = CHUNK * BLK
        peak = None
        for n in range(PART // CHUNK):
            keys = kc[q, n * width : (n + 1) * width, :]
            scores = lax.dot_general(q4, keys, (((1,), (1,)), ((), ())), preferred_element_type=jnp.float32)
            for k in range(CHUNK):
                slot = part * PART + n * CHUNK + k
                block = list_ref[2 * y + q, slot]
                reach = jnp.where(block == my_block, 0, BLK)
                reach = jnp.where(slot < count, reach, -BLK)
                ok = delta <= reach
                tile = scores[:, k * BLK : (k + 1) * BLK].reshape(QH, BLK, BLK)
                tile = jnp.where(ok[None], tile, MASKED).reshape(QH * BLK, BLK)
                s_ref[:, (n * CHUNK + k) * BLK : (n * CHUNK + k + 1) * BLK] = tile
                peak = tile if peak is None else jnp.maximum(peak, tile)
        top = jnp.max(peak, axis=1, keepdims=True)
        total = None
        acc = None
        for n in range(PART // CHUNK):
            weights = jnp.exp2((s_ref[:, n * width : (n + 1) * width] - top) * FACTOR)
            for k in range(CHUNK):
                tile = weights[:, k * BLK : (k + 1) * BLK]
                total = tile if total is None else total + tile
            values = vc[q, n * width : (n + 1) * width, :]
            out = jnp.dot(weights.astype(jnp.bfloat16), values, preferred_element_type=jnp.float32)
            acc = out if acc is None else acc + out
        return top, jnp.sum(total, axis=1, keepdims=True), acc

    load_part(1)
    q_copy.wait()

    def first(q, _):
        top, total, acc = attend(q, 1)
        acc_ref[q] = acc
        m_ref[q] = jnp.broadcast_to(top, (QH * BLK, HD))
        l_ref[q] = jnp.broadcast_to(total, (QH * BLK, HD))
        return 0

    lax.fori_loop(0, 1, first, 0)

    @pl.when(z >= 3)
    def _():
        for i in (1, 3, 2):
            region = vbuf.at[c, (x + 4 - i) % 4, y]
            remote(region, region, vx_send.at[i - 1], vx_recv.at[i - 1], sibling).wait_recv()
        for i in (1, 3, 2):
            vy_copy(i).start()

    lax.fori_loop(1, 2, first, 0)

    @pl.when(z >= 3)
    def _():
        for i in (1, 3, 2):
            region = vbuf.at[c, :, (y + 4 - i) % 4]
            remote(region, region, vy_send.at[i - 1], vy_recv.at[i - 1], sibling).wait_recv()
        vs_copy(c).start()
        vs_copy(1 - c).wait_recv()
        for q in range(2):
            kc[q] = vbuf[0].reshape(PART * BLK, HD)
            vc[q] = vbuf[1].reshape(PART * BLK, HD)

    @pl.when(z < 3)
    def _():
        load_part(0)

    def second(q, _):
        top2, total2, acc2 = attend(q, 0)
        top1 = m_ref[q]
        top = jnp.maximum(top1, top2)
        f1 = jnp.exp2((top1 - top) * FACTOR)
        f2 = jnp.exp2((top2 - top) * FACTOR)
        whole = (f1 * acc_ref[q] + f2 * acc2) / (f1 * l_ref[q] + f2 * total2)
        whole = whole.astype(jnp.bfloat16)
        rows = pl.ds(pl.multiple_of(q * BLK, BLK), BLK)
        for h in range(QH):
            out_ref[rows, h * HD : (h + 1) * HD] = whole[h * BLK : (h + 1) * BLK]
        return 0

    lax.fori_loop(0, 2, second, 0)

    for d in range(3):
        for kv in range(2):

            @pl.when((z_plane(d) <= 7) & jnp.logical_not(z_self(kv, d)))
            def _():
                z_copy(kv, d).wait_send()

    for hi in range(3):
        for kv in range(2):
            for i in range(1, 4):

                @pl.when(p1_live(kv, hi, i))
                def _():
                    p1_copy(kv, hi, i).wait_send()

                @pl.when(p2_live(kv, hi, i))
                def _():
                    p2_copy(kv, hi, i).wait_send()

            for g in range(4):

                @pl.when(needed(hi, g, x))
                def _():
                    sib_copy(kv, hi, g).wait_send()

    @pl.when(z == 2)
    def _():
        for i in range(5):
            vz_copy(i).wait_send()

    @pl.when(z >= 3)
    def _():
        for i in range(1, 4):
            vx_copy(i).wait_send()
            vy_copy(i).wait_send()
        vs_copy(c).wait_send()


def local_attention(queries, key_cache, value_cache, block_list, block_count):
    dma = pltpu.SemaphoreType.DMA
    rows = queries.shape[0] // 4
    return pl.pallas_call(
        attention_kernel,
        out_shape=jax.ShapeDtypeStruct((rows, QH * HD), jnp.bfloat16),
        in_specs=[
            pl.BlockSpec(memory_space=pltpu.SMEM),
            pl.BlockSpec(memory_space=pltpu.SMEM),
            pl.BlockSpec(memory_space=pl.ANY),
            pl.BlockSpec(memory_space=pl.ANY),
            pl.BlockSpec(memory_space=pl.ANY),
        ],
        out_specs=pl.BlockSpec(memory_space=pltpu.VMEM),
        scratch_shapes=[
            pltpu.VMEM((2, 3, 4, 4, 2, 2, BLK, HD), jnp.bfloat16),
            pltpu.VMEM((2, 4, 4, BLK, HD), jnp.bfloat16),
            pltpu.VMEM((2 * BLK, QH * HD), jnp.bfloat16),
            pltpu.VMEM((2, PART * BLK, HD), jnp.bfloat16),
            pltpu.VMEM((2, PART * BLK, HD), jnp.bfloat16),
            pltpu.VMEM((QH * BLK, PART * BLK), jnp.float32),
            pltpu.VMEM((2, QH * BLK, HD), jnp.float32),
            pltpu.VMEM((2, QH * BLK, HD), jnp.float32),
            pltpu.VMEM((2, QH * BLK, HD), jnp.float32),
            dma,
            dma((2, 3)), dma((2, 3)),
            dma((2, 3, 3)), dma((2, 3, 3)),
            dma((2, 3, 3)), dma((2, 3, 3)),
            dma((2, 3, 4)), dma((2, 3, 4)),
            dma((5,)), dma,
            dma((3,)), dma((3,)),
            dma((3,)), dma((3,)),
            dma, dma,
        ],
        compiler_params=pltpu.CompilerParams(has_side_effects=True, vmem_limit_bytes=44 * 1024 * 1024),
    )(block_list, block_count, queries, key_cache.reshape(2, BLK, HD), value_cache.reshape(2, BLK, HD))


def solution(mesh):
    placed = (P("pb", None), P(("ka", "pb"), None), P(("ka", "pb"), None), P("pb", None), P("pb"))
    return jax.shard_map(
        local_attention, mesh=mesh, in_specs=placed, out_specs=P(("pb", "ka"), None), check_vma=False
    )
```

```python
import functools
import math

import jax
import jax.numpy as jnp
from jax import lax
from jax.experimental import pallas as pl
from jax.experimental.pallas import tpu as pltpu
from jax.sharding import PartitionSpec as P

HD = 128
QH = 4
BLK = 128
LIST = 32
NV = 16
PART = 16
CHUNK = 4
MASKED = -1e30
FACTOR = math.log2(math.e) / math.sqrt(HD)


def attention_kernel(
    list_hbm, count_hbm, q_hbm, k_hbm, v_hbm, out_ref,
    list_ref, count_ref, pick_ref,
    buf, vbuf, qs, kc, vc, s_ref, acc_ref, m_ref, l_ref, part_out, part_in, half_out, half_in,
    in_sem, z_send, z_recv, f_send, p1_send, p1_recv, p2_send, p2_recv, sib_send, sib_recv,
    vp_send, vp_recv, vh_send, vh_recv, vz_send, vz_recv, v1_send, v1_recv, v2_send, v2_recv, vs_send, vs_recv,
):
    p = lax.axis_index("pb")
    y = lax.axis_index("ka")
    z = p // 8
    x = (p // 2) % 4
    c = p % 2

    def dev(zz, xx, cc, yy):
        return (zz * 8 + xx * 2 + cc, yy)

    def remote(src, dst, ssem, rsem, device):
        return pltpu.make_async_remote_copy(
            src_ref=src, dst_ref=dst, send_sem=ssem, recv_sem=rsem,
            device_id=device, device_id_type=pl.DeviceIdType.MESH,
        )

    def have(hi):
        return z >= 2 - hi

    def needed(hi, g, xx):
        if hi == 1:
            return have(hi)
        if hi == 0:
            return have(hi) & (g >= xx)
        return g <= xx

    inputs = [
        pltpu.make_async_copy(list_hbm, list_ref, in_sem.at[0]),
        pltpu.make_async_copy(count_hbm, count_ref, in_sem.at[1]),
        pltpu.make_async_copy(q_hbm.at[pl.ds(pl.multiple_of(y * 256, 256), 256)], qs, in_sem.at[2]),
    ]
    for copy in inputs:
        copy.start()

    src = (k_hbm, v_hbm)
    g_own = z % 4
    half = 2 * y + z // 4
    z_plane = jnp.minimum(half + 1, 7)
    z_half = jnp.where(half == 7, 2, 1)

    def z_target(kv):
        xd, yd = (x, g_own) if kv == 0 else (g_own, x)
        return z_plane, xd, c, yd

    def z_source(kv, h):
        return (4 * (h % 2) + y, x, c, h // 2) if kv == 0 else (4 * (h % 2) + x, y, c, h // 2)

    def here(device):
        zz, xx, _, yy = device
        return (zz == z) & (xx == x) & (yy == y)

    barrier = pltpu.get_barrier_semaphore()
    partners = []
    always = z >= 0
    for i in range(1, 4):
        partners.append((always, (z, (x + i) % 4, c, y)))
        partners.append((always, (z, x, c, (y + i) % 4)))
    partners.append((always, (z, x, 1 - c, y)))
    partners.append((z >= 1, (jnp.maximum(z - 1, 0), x, c, y)))
    partners.append((z <= 6, (jnp.minimum(z + 1, 7), x, c, y)))
    for i in range(5):
        partners.append((z == 2, (3 + i, x, c, y)))
    partners.append((z >= 3, (2, x, c, y)))
    for kv in range(2):
        there = z_target(kv)
        partners.append((jnp.logical_not(here(there)), there))
        there = z_source(kv, jnp.maximum(z - 1, 0))
        partners.append(((z >= 1) & jnp.logical_not(here(there)), there))
        there = z_source(kv, 7)
        partners.append(((z == 7) & jnp.logical_not(here(there)), there))
    expected = jnp.int32(0)
    for live, there in partners:

        @pl.when(live)
        def _():
            pl.semaphore_signal(barrier, inc=1, device_id=dev(*there), device_id_type=pl.DeviceIdType.MESH)

        expected = expected + jnp.where(live, 1, 0)
    pl.semaphore_wait(barrier, expected)

    def z_copy(kv):
        region = buf.at[kv, z_half, g_own, x, c]
        return remote(src[kv], region, z_send.at[kv], z_recv.at[kv, z_half], dev(*z_target(kv)))

    for kv in range(2):
        own = here(z_target(kv))

        @pl.when(jnp.logical_not(own))
        def _():
            z_copy(kv).start()

        @pl.when(own)
        def _():
            pltpu.make_async_copy(src[kv], buf.at[kv, z_half, g_own, x, c], z_recv.at[kv, z_half]).start()

    def row(kv):
        return y if kv == 0 else x

    def col(kv):
        return x if kv == 0 else y

    def along(kv, i):
        return dev(z, (x + i) % 4, c, y) if kv == 0 else dev(z, x, c, (y + i) % 4)

    def across(kv, i):
        return dev(z, x, c, (y + i) % 4) if kv == 0 else dev(z, (x + i) % 4, c, y)

    sibling = dev(z, x, 1 - c, y)

    def p1_copy(kv, hi, i):
        region = buf.at[kv, hi, row(kv), col(kv), c]
        return remote(region, region, p1_send.at[kv, hi, i - 1], p1_recv.at[kv, hi, i - 1], along(kv, i))

    def p1_live(kv, hi, i):
        if kv == 1:
            return have(hi)
        wanted = needed(hi, y, (x + i) % 4)
        return wanted | (z == 2) if hi == 0 else wanted

    def p1_got(kv, hi):
        if kv == 1:
            return have(hi)
        wanted = needed(hi, y, x)
        return wanted | (z == 2) if hi == 0 else wanted

    def p2_copy(kv, hi, i):
        region = buf.at[kv, hi, row(kv), :, c]
        return remote(region, region, p2_send.at[kv, hi, i - 1], p2_recv.at[kv, hi, i - 1], across(kv, i))

    def p2_live(kv, hi, i):
        return needed(hi, y, x) if kv == 0 else needed(hi, x, (x + i) % 4)

    def sib_copy(kv, hi, g):
        region = buf.at[kv, hi, g, :, c]
        return remote(region, region, sib_send.at[kv, hi, g], sib_recv.at[kv, hi, g], sibling)

    def vz_copy(i):
        return remote(vbuf.at[c, x, y], vbuf.at[c, x, y], vz_send.at[i], vz_recv, dev(3 + i, x, c, y))

    def v_line(first, i):
        to_x = (c == 0) == first
        return dev(z, jnp.where(to_x, (x + i) % 4, x), c, jnp.where(to_x, y, (y + i) % 4))

    def v1_copy(i):
        return remote(vbuf.at[c, x, y], vbuf.at[c, x, y], v1_send.at[i - 1], v1_recv.at[i - 1], v_line(True, i))

    def v2_copy(cc, i):
        region = vbuf.at[0, :, y] if cc == 0 else vbuf.at[1, x]
        return remote(region, region, v2_send.at[i - 1], v2_recv.at[i - 1], v_line(False, i))

    def vs_copy(cc):
        return remote(vbuf.at[cc], vbuf.at[cc], vs_send, vs_recv, sibling)

    def f_copy(kv, up):
        region = buf.at[kv, 1, row(kv), col(kv), c]
        there = buf.at[kv, 0 if up else 2, row(kv), col(kv), c]
        to = jnp.minimum(z + 1, 7) if up else jnp.maximum(z - 1, 0)
        return remote(region, there, f_send.at[kv, int(up)], z_recv.at[kv, 0 if up else 2], dev(to, x, c, y))

    def f_live(up):
        return (z >= 1) & (z <= 6) if up else z >= 1

    for copy in inputs[:2]:
        copy.wait()

    @pl.when(z == 2)
    def _():
        entries = [list_ref[2 * y, i] for i in range(NV)]
        slots = [4 * x + (y + i) % 4 for i in range(4)] + [4 * ((x + i) % 4) + y for i in range(4)]
        chosen = [jnp.int32(-1)] * 8
        for i in range(NV):
            rank = jnp.int32(0)
            for j in range(NV):
                if j != i:
                    rank = rank + jnp.where(entries[j] < entries[i], 1, 0)
            chosen = [jnp.where(rank == slot, entries[i], now) for slot, now in zip(slots, chosen)]
        for n in range(8):
            pick_ref[n] = chosen[n]

    for hi in (1, 2, 0):
        for kv in range(2):

            @pl.when(have(hi))
            def _():
                pltpu.make_async_copy(src[kv], buf.at[kv, hi, row(kv), col(kv), c], z_recv.at[kv, hi]).wait()

            if hi == 1:
                for up in (False, True):

                    @pl.when(f_live(up))
                    def _():
                        f_copy(kv, up).start()

            for i in (1, 3, 2):

                @pl.when(p1_live(kv, hi, i))
                def _():
                    p1_copy(kv, hi, i).start()

    def p1_wait(hi):
        for kv in range(2):
            for i in (1, 3, 2):

                @pl.when(p1_got(kv, hi))
                def _():
                    region = buf.at[kv, hi, row(kv), (col(kv) + 4 - i) % 4, c]
                    remote(region, region, p1_send.at[kv, hi, i - 1], p1_recv.at[kv, hi, i - 1], sibling).wait_recv()

    def p2_start(hi, when):
        for kv in range(2):
            for i in (1, 3, 2):

                @pl.when(p2_live(kv, hi, i) & when)
                def _():
                    p2_copy(kv, hi, i).start()

            @pl.when(needed(hi, row(kv), x) & when)
            def _():
                sib_copy(kv, hi, row(kv)).start()

    def collect(hi):
        for i in (1, 3, 2):
            for kv in range(2):
                g = (row(kv) + 4 - i) % 4

                @pl.when(needed(hi, g, x))
                def _():
                    region = buf.at[kv, hi, g, :, c]
                    remote(region, region, p2_send.at[kv, hi, i - 1], p2_recv.at[kv, hi, i - 1], sibling).wait_recv()
                    sib_copy(kv, hi, g).start()

    def vp_copy(kv, i):
        return remote(
            part_out.at[kv, i], part_in.at[kv, i - 1], vp_send.at[kv, i - 1], vp_recv.at[kv, i - 1], across(kv, i)
        )

    def vh_copy(kv):
        return remote(half_out.at[kv], half_in, vh_send, vh_recv, sibling)

    p1_wait(1)
    p2_start(1, z != 2)
    p1_wait(2)
    p1_wait(0)

    @pl.when(z == 2)
    def _():
        for kv in range(2):

            def pick(n, _):
                l, r, hi = n // 4, (n // 2) % 2, n % 2
                block = buf[kv, hi, row(kv), l, c, r]
                name = 64 * hi + 16 * row(kv) + 4 * l + 2 * c + r
                for i in range(4):
                    part_out[kv, i] = jnp.where(pick_ref[4 * kv + i] == name, block, part_out[kv, i])
                return 0

            part_out[kv] = jnp.zeros((4, BLK, HD), jnp.bfloat16)
            lax.fori_loop(0, 16, pick, 0)
            for i in (1, 3, 2):
                vp_copy(kv, i).start()

    p2_start(1, z == 2)
    p2_start(2, z >= 0)

    @pl.when(z == 2)
    def _():
        for kv in range(2):
            for i in (1, 3, 2):
                vp_copy(kv, i).wait_recv()
            half_out[kv] = (part_out[kv, 0] + part_in[kv, 0]) + (part_in[kv, 1] + part_in[kv, 2])
        vh_copy(1 - c).start()
        vh_copy(c).wait_recv()
        vbuf[c, x, y] = half_out[c] + half_in[...]
        for i in (0, 4, 1, 3, 2):
            vz_copy(i).start()

    @pl.when(z >= 3)
    def _():
        vz_copy(0).wait_recv()

    @pl.when(z >= 2)
    def _():
        for i in (1, 3, 2):
            v1_copy(i).start()
        for i in (1, 3, 2):
            v1_copy(i).wait_recv()
        for cc in range(2):

            @pl.when(c == cc)
            def _():
                for i in (1, 3, 2):
                    v2_copy(cc, i).start()

    p2_start(0, z >= 0)
    collect(1)
    collect(2)

    @pl.when(z >= 2)
    def _():
        for cc in range(2):

            @pl.when(c == cc)
            def _():
                for i in (1, 3, 2):
                    v2_copy(cc, i).wait_recv()
                vs_copy(cc).start()
                vs_copy(1 - cc).wait_recv()

    def place(block):
        rel = jnp.clip(block - 64 * (z - 2), 0, 191)
        return rel >> 6, (rel >> 4) & 3, (rel >> 2) & 3, (rel >> 1) & 1, rel & 1

    def block_of(kv, block):
        hi, g, l, cc, r = place(block)
        return buf[kv, hi, g, l, cc, r]

    delta = lax.broadcasted_iota(jnp.int32, (BLK, BLK), 1) - lax.broadcasted_iota(jnp.int32, (BLK, BLK), 0)

    def load_part(part):
        def load(n, _):
            q = n // PART
            s = n % PART
            block = list_ref[2 * y + q, part * PART + s]
            rows = pl.ds(pl.multiple_of(s * BLK, BLK), BLK)
            kc[q, rows, :] = block_of(0, block)
            vc[q, rows, :] = block_of(1, block)
            return 0

        lax.fori_loop(0, 2 * PART, load, 0)

    def keys_of(q, part, masked, n):
        if masked:
            return kc[q, n * CHUNK * BLK : (n + 1) * CHUNK * BLK, :]
        return vbuf[0, n].reshape(CHUNK * BLK, HD)

    def values_of(q, part, masked, n):
        if masked:
            return vc[q, n * CHUNK * BLK : (n + 1) * CHUNK * BLK, :]
        return vbuf[1, n].reshape(CHUNK * BLK, HD)

    def attend(q, part, masked=True):
        my_block = 8 * p + 2 * y + q
        count = count_ref[2 * y + q]
        rows = pl.ds(pl.multiple_of(q * BLK, BLK), BLK)
        q4 = jnp.concatenate([qs[rows, h * HD : (h + 1) * HD] for h in range(QH)], axis=0)
        width = CHUNK * BLK
        peak = None
        for n in range(PART // CHUNK):
            keys = keys_of(q, part, masked, n)
            scores = lax.dot_general(q4, keys, (((1,), (1,)), ((), ())), preferred_element_type=jnp.float32)
            for k in range(CHUNK):
                if not masked:
                    tile = scores[:, k * BLK : (k + 1) * BLK]
                    peak = tile if peak is None else jnp.maximum(peak, tile)
                    continue
                slot = part * PART + n * CHUNK + k
                block = list_ref[2 * y + q, slot]
                reach = jnp.where(block == my_block, 0, BLK)
                reach = jnp.where(slot < count, reach, -BLK)
                ok = delta <= reach
                tile = scores[:, k * BLK : (k + 1) * BLK].reshape(QH, BLK, BLK)
                tile = jnp.where(ok[None], tile, MASKED).reshape(QH * BLK, BLK)
                s_ref[:, (n * CHUNK + k) * BLK : (n * CHUNK + k + 1) * BLK] = tile
                peak = tile if peak is None else jnp.maximum(peak, tile)
            if not masked:
                s_ref[:, n * width : (n + 1) * width] = scores
        top = jnp.max(peak, axis=1, keepdims=True)
        total = None
        acc = None
        for n in range(PART // CHUNK):
            weights = jnp.exp2((s_ref[:, n * width : (n + 1) * width] - top) * FACTOR)
            for k in range(CHUNK):
                tile = weights[:, k * BLK : (k + 1) * BLK]
                total = tile if total is None else total + tile
            values = values_of(q, part, masked, n)
            out = jnp.dot(weights.astype(jnp.bfloat16), values, preferred_element_type=jnp.float32)
            acc = out if acc is None else acc + out
        return top, jnp.sum(total, axis=1, keepdims=True), acc

    def first(q, masked):
        top, total, acc = attend(q, 0, masked)
        acc_ref[q] = acc
        m_ref[q] = jnp.broadcast_to(top, (QH * BLK, HD))
        l_ref[q] = jnp.broadcast_to(total, (QH * BLK, HD))

    inputs[2].wait()

    @pl.when(z >= 2)
    def _():
        def early(q, _):
            first(q, False)
            return 0

        lax.fori_loop(0, 2, early, 0)

    collect(0)
    for hi in (1, 2, 0):
        for kv in range(2):
            for g in range(4):

                @pl.when(needed(hi, g, x))
                def _():
                    region = buf.at[kv, hi, g, :, 1 - c]
                    remote(region, region, sib_send.at[kv, hi, g], sib_recv.at[kv, hi, g], sibling).wait_recv()

    @pl.when(z < 2)
    def _():
        load_part(0)

        def late(q, _):
            first(q, True)
            return 0

        lax.fori_loop(0, 2, late, 0)

    load_part(1)

    def second(q, _):
        top2, total2, acc2 = attend(q, 1)
        top1 = m_ref[q]
        top = jnp.maximum(top1, top2)
        f1 = jnp.exp2((top1 - top) * FACTOR)
        f2 = jnp.exp2((top2 - top) * FACTOR)
        whole = (f1 * acc_ref[q] + f2 * acc2) / (f1 * l_ref[q] + f2 * total2)
        whole = whole.astype(jnp.bfloat16)
        rows = pl.ds(pl.multiple_of(q * BLK, BLK), BLK)
        for h in range(QH):
            out_ref[rows, h * HD : (h + 1) * HD] = whole[h * BLK : (h + 1) * BLK]
        return 0

    lax.fori_loop(0, 2, second, 0)

    for kv in range(2):

        @pl.when(jnp.logical_not(here(z_target(kv))))
        def _():
            z_copy(kv).wait_send()

        for up in (False, True):

            @pl.when(f_live(up))
            def _():
                f_copy(kv, up).wait_send()

    for hi in range(3):
        for kv in range(2):
            for i in range(1, 4):

                @pl.when(p1_live(kv, hi, i))
                def _():
                    p1_copy(kv, hi, i).wait_send()

                @pl.when(p2_live(kv, hi, i))
                def _():
                    p2_copy(kv, hi, i).wait_send()

            for g in range(4):

                @pl.when(needed(hi, g, x))
                def _():
                    sib_copy(kv, hi, g).wait_send()

    @pl.when(z == 2)
    def _():
        for kv in range(2):
            for i in range(1, 4):
                vp_copy(kv, i).wait_send()
        vh_copy(1 - c).wait_send()
        for i in range(5):
            vz_copy(i).wait_send()

    @pl.when(z >= 2)
    def _():
        for i in range(1, 4):
            v1_copy(i).wait_send()
        for cc in range(2):

            @pl.when(c == cc)
            def _():
                for i in range(1, 4):
                    v2_copy(cc, i).wait_send()
                vs_copy(cc).wait_send()


def local_attention(queries, key_cache, value_cache, block_list, block_count):
    dma = pltpu.SemaphoreType.DMA
    rows = queries.shape[0] // 4
    return pl.pallas_call(
        attention_kernel,
        out_shape=jax.ShapeDtypeStruct((rows, QH * HD), jnp.bfloat16),
        in_specs=[
            pl.BlockSpec(memory_space=pl.ANY),
            pl.BlockSpec(memory_space=pl.ANY),
            pl.BlockSpec(memory_space=pl.ANY),
            pl.BlockSpec(memory_space=pl.ANY),
            pl.BlockSpec(memory_space=pl.ANY),
        ],
        out_specs=pl.BlockSpec(memory_space=pltpu.VMEM),
        scratch_shapes=[
            pltpu.SMEM((8, LIST), jnp.int32),
            pltpu.SMEM((8,), jnp.int32),
            pltpu.SMEM((8,), jnp.int32),
            pltpu.VMEM((2, 3, 4, 4, 2, 2, BLK, HD), jnp.bfloat16),
            pltpu.VMEM((2, 4, 4, BLK, HD), jnp.bfloat16),
            pltpu.VMEM((2 * BLK, QH * HD), jnp.bfloat16),
            pltpu.VMEM((2, PART * BLK, HD), jnp.bfloat16),
            pltpu.VMEM((2, PART * BLK, HD), jnp.bfloat16),
            pltpu.VMEM((QH * BLK, PART * BLK), jnp.float32),
            pltpu.VMEM((2, QH * BLK, HD), jnp.float32),
            pltpu.VMEM((2, QH * BLK, HD), jnp.float32),
            pltpu.VMEM((2, QH * BLK, HD), jnp.float32),
            pltpu.VMEM((2, 4, BLK, HD), jnp.bfloat16),
            pltpu.VMEM((2, 3, BLK, HD), jnp.bfloat16),
            pltpu.VMEM((2, BLK, HD), jnp.bfloat16),
            pltpu.VMEM((BLK, HD), jnp.bfloat16),
            dma((3,)),
            dma((2,)), dma((2, 3)), dma((2, 2)),
            dma((2, 3, 3)), dma((2, 3, 3)),
            dma((2, 3, 3)), dma((2, 3, 3)),
            dma((2, 3, 4)), dma((2, 3, 4)),
            dma((2, 3)), dma((2, 3)),
            dma, dma,
            dma((5,)), dma,
            dma((3,)), dma((3,)),
            dma((3,)), dma((3,)),
            dma, dma,
        ],
        compiler_params=pltpu.CompilerParams(collective_id=0, has_side_effects=True, vmem_limit_bytes=60 * 1024 * 1024),
    )(block_list, block_count, queries, key_cache.reshape(2, BLK, HD), value_cache.reshape(2, BLK, HD))


def solution(mesh):
    placed = (P("pb", None), P(("ka", "pb"), None), P(("ka", "pb"), None), P("pb", None), P("pb"))
    return jax.shard_map(
        local_attention, mesh=mesh, in_specs=placed, out_specs=P(("pb", "ka"), None), check_vma=False
    )
```

```python
import functools
import math

import jax
import jax.numpy as jnp
from jax import lax
from jax.experimental import pallas as pl
from jax.experimental.pallas import tpu as pltpu
from jax.sharding import PartitionSpec as P

HD = 128
QH = 4
BLK = 128
LIST = 32
NV = 16
PART = 16
CHUNK = 4
MASKED = -1e30
FACTOR = math.log2(math.e) / math.sqrt(HD)


def attention_kernel(
    list_hbm, count_hbm, q_hbm, k_hbm, v_hbm, out_ref,
    list_ref, count_ref, pick_ref,
    buf, vbuf, qs, kc, vc, s_ref, acc_ref, m_ref, l_ref, part_out, part_in, half_out, half_in,
    in_sem, z_send, z_recv, f_send, p1_send, p1_recv, p2_send, p2_recv, f2_send, f2_recv, sib_send, sib_recv,
    vp_send, vp_recv, vh_send, vh_recv, vz_send, vz_recv, v1_send, v1_recv, v2_send, v2_recv, vs_send, vs_recv,
):
    p = lax.axis_index("pb")
    y = lax.axis_index("ka")
    z = p // 8
    x = (p // 2) % 4
    c = p % 2

    def dev(zz, xx, cc, yy):
        return (zz * 8 + xx * 2 + cc, yy)

    def remote(src, dst, ssem, rsem, device):
        return pltpu.make_async_remote_copy(
            src_ref=src, dst_ref=dst, send_sem=ssem, recv_sem=rsem,
            device_id=device, device_id_type=pl.DeviceIdType.MESH,
        )

    def have(hi):
        return z >= 2 - hi

    def needed(hi, g, xx):
        if hi == 1:
            return have(hi)
        if hi == 0:
            return have(hi) & (g >= xx)
        return g <= xx

    inputs = [
        pltpu.make_async_copy(list_hbm, list_ref, in_sem.at[0]),
        pltpu.make_async_copy(count_hbm, count_ref, in_sem.at[1]),
        pltpu.make_async_copy(q_hbm.at[pl.ds(pl.multiple_of(y * 256, 256), 256)], qs, in_sem.at[2]),
    ]
    for copy in inputs:
        copy.start()

    src = (k_hbm, v_hbm)
    g_own = z % 4
    half = 2 * y + z // 4
    z_plane = jnp.minimum(half + 1, 7)
    z_half = jnp.where(half == 7, 2, 1)

    def z_target(kv):
        xd, yd = (x, g_own) if kv == 0 else (g_own, x)
        return z_plane, xd, c, yd

    def z_source(kv, h):
        return (4 * (h % 2) + y, x, c, h // 2) if kv == 0 else (4 * (h % 2) + x, y, c, h // 2)

    def here(device):
        zz, xx, _, yy = device
        return (zz == z) & (xx == x) & (yy == y)

    barrier = pltpu.get_barrier_semaphore()
    partners = []
    always = z >= 0
    for i in range(1, 4):
        partners.append((always, (z, (x + i) % 4, c, y)))
        partners.append((always, (z, x, c, (y + i) % 4)))
    partners.append((always, (z, x, 1 - c, y)))
    partners.append((z >= 1, (jnp.maximum(z - 1, 0), x, c, y)))
    partners.append((z <= 6, (jnp.minimum(z + 1, 7), x, c, y)))
    for i in range(5):
        partners.append((z == 2, (3 + i, x, c, y)))
    partners.append((z >= 3, (2, x, c, y)))
    for kv in range(2):
        there = z_target(kv)
        partners.append((jnp.logical_not(here(there)), there))
        there = z_source(kv, jnp.maximum(z - 1, 0))
        partners.append(((z >= 1) & jnp.logical_not(here(there)), there))
        there = z_source(kv, 7)
        partners.append(((z == 7) & jnp.logical_not(here(there)), there))
    expected = jnp.int32(0)
    for live, there in partners:

        @pl.when(live)
        def _():
            pl.semaphore_signal(barrier, inc=1, device_id=dev(*there), device_id_type=pl.DeviceIdType.MESH)

        expected = expected + jnp.where(live, 1, 0)
    pl.semaphore_wait(barrier, expected)

    def z_copy(kv):
        region = buf.at[kv, z_half, g_own, x, c]
        return remote(src[kv], region, z_send.at[kv], z_recv.at[kv, z_half], dev(*z_target(kv)))

    for kv in range(2):
        own = here(z_target(kv))

        @pl.when(jnp.logical_not(own))
        def _():
            z_copy(kv).start()

        @pl.when(own)
        def _():
            pltpu.make_async_copy(src[kv], buf.at[kv, z_half, g_own, x, c], z_recv.at[kv, z_half]).start()

    def row(kv):
        return y if kv == 0 else x

    def col(kv):
        return x if kv == 0 else y

    def along(kv, i):
        return dev(z, (x + i) % 4, c, y) if kv == 0 else dev(z, x, c, (y + i) % 4)

    def across(kv, i):
        return dev(z, x, c, (y + i) % 4) if kv == 0 else dev(z, (x + i) % 4, c, y)

    sibling = dev(z, x, 1 - c, y)

    def p1_copy(kv, hi, i):
        region = buf.at[kv, hi, row(kv), col(kv), c]
        return remote(region, region, p1_send.at[kv, hi, i - 1], p1_recv.at[kv, hi, i - 1], along(kv, i))

    def p1_live(kv, hi, i):
        if kv == 1:
            return have(hi)
        wanted = needed(hi, y, (x + i) % 4)
        return wanted | (z == 2) if hi == 0 else wanted

    def p1_got(kv, hi):
        if kv == 1:
            return have(hi)
        wanted = needed(hi, y, x)
        return wanted | (z == 2) if hi == 0 else wanted

    def p2_copy(kv, hi, i):
        region = buf.at[kv, hi, row(kv), :, c]
        return remote(region, region, p2_send.at[kv, hi, i - 1], p2_recv.at[kv, hi, i - 1], across(kv, i))

    def relayed(kv, hi):
        return kv == 0 or hi == 1

    def far_copy(kv, hi, i):
        g, first = (row(kv) + 4 - i) % 4, 0 if i == 1 else 2
        region = buf.at[kv, hi, g, first : first + 2, c]
        return remote(region, region, f2_send.at[kv, hi, i // 2], f2_recv.at[kv, hi, i // 2], across(kv, i))

    def p2_live(kv, hi, i):
        return needed(hi, y, x) if kv == 0 else needed(hi, x, (x + i) % 4)

    def sib_copy(kv, hi, g):
        region = buf.at[kv, hi, g, :, c]
        return remote(region, region, sib_send.at[kv, hi, g], sib_recv.at[kv, hi, g], sibling)

    def vz_copy(i):
        return remote(vbuf.at[c, x, y], vbuf.at[c, x, y], vz_send.at[i], vz_recv, dev(3 + i, x, c, y))

    def v_line(first, i):
        to_x = (c == 0) == first
        return dev(z, jnp.where(to_x, (x + i) % 4, x), c, jnp.where(to_x, y, (y + i) % 4))

    def v1_copy(i):
        return remote(vbuf.at[c, x, y], vbuf.at[c, x, y], v1_send.at[i - 1], v1_recv.at[i - 1], v_line(True, i))

    def v2_copy(cc, i):
        region = vbuf.at[0, :, y] if cc == 0 else vbuf.at[1, x]
        return remote(region, region, v2_send.at[i - 1], v2_recv.at[i - 1], v_line(False, i))

    def vs_copy(cc):
        return remote(vbuf.at[cc], vbuf.at[cc], vs_send, vs_recv, sibling)

    def f_copy(kv, up):
        region = buf.at[kv, 1, row(kv), col(kv), c]
        there = buf.at[kv, 0 if up else 2, row(kv), col(kv), c]
        to = jnp.minimum(z + 1, 7) if up else jnp.maximum(z - 1, 0)
        return remote(region, there, f_send.at[kv, int(up)], z_recv.at[kv, 0 if up else 2], dev(to, x, c, y))

    def f_live(up):
        return (z >= 1) & (z <= 6) if up else z >= 1

    for copy in inputs[:2]:
        copy.wait()

    @pl.when(z == 2)
    def _():
        entries = [list_ref[2 * y, i] for i in range(NV)]
        slots = [4 * x + (y + i) % 4 for i in range(4)] + [4 * ((x + i) % 4) + y for i in range(4)]
        chosen = [jnp.int32(-1)] * 8
        for i in range(NV):
            rank = jnp.int32(0)
            for j in range(NV):
                if j != i:
                    rank = rank + jnp.where(entries[j] < entries[i], 1, 0)
            chosen = [jnp.where(rank == slot, entries[i], now) for slot, now in zip(slots, chosen)]
        for n in range(8):
            pick_ref[n] = chosen[n]

    for hi in (1, 0, 2):
        for kv in range(2):

            @pl.when(have(hi))
            def _():
                pltpu.make_async_copy(src[kv], buf.at[kv, hi, row(kv), col(kv), c], z_recv.at[kv, hi]).wait()

            if hi == 1:
                for up in (False, True):

                    @pl.when(f_live(up))
                    def _():
                        f_copy(kv, up).start()

            for i in (1, 3, 2):

                @pl.when(p1_live(kv, hi, i))
                def _():
                    p1_copy(kv, hi, i).start()

    def p1_wait(hi):
        for kv in range(2):
            for i in (1, 3, 2):

                @pl.when(p1_got(kv, hi))
                def _():
                    region = buf.at[kv, hi, row(kv), (col(kv) + 4 - i) % 4, c]
                    remote(region, region, p1_send.at[kv, hi, i - 1], p1_recv.at[kv, hi, i - 1], sibling).wait_recv()

    def p2_start(hi, when):
        for kv in range(2):
            for i in (1, 3) if relayed(kv, hi) else (1, 3, 2):

                @pl.when(p2_live(kv, hi, i) & when)
                def _():
                    p2_copy(kv, hi, i).start()

            @pl.when(needed(hi, row(kv), x) & when)
            def _():
                sib_copy(kv, hi, row(kv)).start()

    def near(hi):
        for i in (1, 3):
            for kv in range(2):
                g = (row(kv) + 4 - i) % 4

                @pl.when(needed(hi, g, x))
                def _():
                    region = buf.at[kv, hi, g, :, c]
                    remote(region, region, p2_send.at[kv, hi, i - 1], p2_recv.at[kv, hi, i - 1], sibling).wait_recv()
                    if relayed(kv, hi):
                        far_copy(kv, hi, i).start()
                    sib_copy(kv, hi, g).start()

    def far(hi):
        for kv in range(2):
            g = (row(kv) + 2) % 4

            @pl.when(needed(hi, g, x))
            def _():
                if relayed(kv, hi):
                    for i in (1, 3):
                        first = 0 if i == 1 else 2
                        region = buf.at[kv, hi, g, first : first + 2, c]
                        remote(region, region, f2_send.at[kv, hi, i // 2], f2_recv.at[kv, hi, i // 2], sibling).wait_recv()
                else:
                    region = buf.at[kv, hi, g, :, c]
                    remote(region, region, p2_send.at[kv, hi, 1], p2_recv.at[kv, hi, 1], sibling).wait_recv()
                sib_copy(kv, hi, g).start()

    def vp_copy(kv, i):
        return remote(
            part_out.at[kv, i], part_in.at[kv, i - 1], vp_send.at[kv, i - 1], vp_recv.at[kv, i - 1], across(kv, i)
        )

    def vh_copy(kv):
        return remote(half_out.at[kv], half_in, vh_send, vh_recv, sibling)

    p1_wait(1)
    p2_start(1, z >= 0)
    p1_wait(0)

    @pl.when(z == 2)
    def _():
        for kv in range(2):

            picked = [jnp.zeros((BLK, HD), jnp.bfloat16)] * 4
            for hi in range(2):
                for l in range(4):
                    for r in range(2):
                        block = buf[kv, hi, row(kv), l, c, r]
                        name = 64 * hi + 16 * row(kv) + 4 * l + 2 * c + r
                        picked = [jnp.where(pick_ref[4 * kv + i] == name, block, picked[i]) for i in range(4)]
            for i in range(4):
                part_out[kv, i] = picked[i]
            for i in (1, 3, 2):
                vp_copy(kv, i).start()

    p2_start(0, z >= 0)
    p1_wait(2)
    p2_start(2, z >= 0)

    @pl.when(z == 2)
    def _():
        for kv in range(2):
            for i in (1, 3, 2):
                vp_copy(kv, i).wait_recv()
            half_out[kv] = (part_out[kv, 0] + part_in[kv, 0]) + (part_in[kv, 1] + part_in[kv, 2])
        vh_copy(1 - c).start()
        vh_copy(c).wait_recv()
        vbuf[c, x, y] = half_out[c] + half_in[...]
        for i in (0, 4, 1, 3, 2):
            vz_copy(i).start()

    near(1)
    near(0)

    @pl.when(z >= 3)
    def _():
        vz_copy(0).wait_recv()

    @pl.when(z >= 2)
    def _():
        for i in (1, 3, 2):
            v1_copy(i).start()

    far(1)
    near(2)

    @pl.when(z >= 2)
    def _():
        for i in (1, 3, 2):
            v1_copy(i).wait_recv()
        for cc in range(2):

            @pl.when(c == cc)
            def _():
                for i in (1, 3, 2):
                    v2_copy(cc, i).start()

    far(0)
    far(2)
    for hi in (1, 0, 2):
        for kv in range(2):
            for g in range(4):

                @pl.when(needed(hi, g, x))
                def _():
                    region = buf.at[kv, hi, g, :, 1 - c]
                    remote(region, region, sib_send.at[kv, hi, g], sib_recv.at[kv, hi, g], sibling).wait_recv()

    def place(block):
        rel = jnp.clip(block - 64 * (z - 2), 0, 191)
        return rel >> 6, (rel >> 4) & 3, (rel >> 2) & 3, (rel >> 1) & 1, rel & 1

    def block_of(kv, block):
        hi, g, l, cc, r = place(block)
        return buf[kv, hi, g, l, cc, r]

    delta = lax.broadcasted_iota(jnp.int32, (BLK, BLK), 1) - lax.broadcasted_iota(jnp.int32, (BLK, BLK), 0)

    def load_part(part):
        def load(n, _):
            q = n // PART
            s = n % PART
            block = list_ref[2 * y + q, part * PART + s]
            rows = pl.ds(pl.multiple_of(s * BLK, BLK), BLK)
            kc[q, rows, :] = block_of(0, block)
            vc[q, rows, :] = block_of(1, block)
            return 0

        lax.fori_loop(0, 2 * PART, load, 0)

    def keys_of(q, part, masked, n):
        if masked:
            return kc[q, n * CHUNK * BLK : (n + 1) * CHUNK * BLK, :]
        return vbuf[0, n].reshape(CHUNK * BLK, HD)

    def values_of(q, part, masked, n):
        if masked:
            return vc[q, n * CHUNK * BLK : (n + 1) * CHUNK * BLK, :]
        return vbuf[1, n].reshape(CHUNK * BLK, HD)

    def attend(q, part, masked=True):
        my_block = 8 * p + 2 * y + q
        count = count_ref[2 * y + q]
        rows = pl.ds(pl.multiple_of(q * BLK, BLK), BLK)
        q4 = jnp.concatenate([qs[rows, h * HD : (h + 1) * HD] for h in range(QH)], axis=0)
        width = CHUNK * BLK
        peak = None
        for n in range(PART // CHUNK):
            keys = keys_of(q, part, masked, n)
            scores = lax.dot_general(q4, keys, (((1,), (1,)), ((), ())), preferred_element_type=jnp.float32)
            for k in range(CHUNK):
                if not masked:
                    tile = scores[:, k * BLK : (k + 1) * BLK]
                    peak = tile if peak is None else jnp.maximum(peak, tile)
                    continue
                slot = part * PART + n * CHUNK + k
                block = list_ref[2 * y + q, slot]
                reach = jnp.where(block == my_block, 0, BLK)
                reach = jnp.where(slot < count, reach, -BLK)
                ok = delta <= reach
                tile = scores[:, k * BLK : (k + 1) * BLK].reshape(QH, BLK, BLK)
                tile = jnp.where(ok[None], tile, MASKED).reshape(QH * BLK, BLK)
                s_ref[:, (n * CHUNK + k) * BLK : (n * CHUNK + k + 1) * BLK] = tile
                peak = tile if peak is None else jnp.maximum(peak, tile)
            if not masked:
                s_ref[:, n * width : (n + 1) * width] = scores
        top = jnp.max(peak, axis=1, keepdims=True)
        total = None
        acc = None
        for n in range(PART // CHUNK):
            weights = jnp.exp2((s_ref[:, n * width : (n + 1) * width] - top) * FACTOR)
            for k in range(CHUNK):
                tile = weights[:, k * BLK : (k + 1) * BLK]
                total = tile if total is None else total + tile
            values = values_of(q, part, masked, n)
            out = jnp.dot(weights.astype(jnp.bfloat16), values, preferred_element_type=jnp.float32)
            acc = out if acc is None else acc + out
        return top, jnp.sum(total, axis=1, keepdims=True), acc

    inputs[2].wait()
    load_part(1)

    def first(q, _):
        top, total, acc = attend(q, 1)
        acc_ref[q] = acc
        m_ref[q] = jnp.broadcast_to(top, (QH * BLK, HD))
        l_ref[q] = jnp.broadcast_to(total, (QH * BLK, HD))
        return 0

    lax.fori_loop(0, 1, first, 0)

    @pl.when(z >= 2)
    def _():
        for cc in range(2):

            @pl.when(c == cc)
            def _():
                for i in (1, 3, 2):
                    v2_copy(cc, i).wait_recv()
                vs_copy(cc).start()

    lax.fori_loop(1, 2, first, 0)

    def second(q, masked):
        top2, total2, acc2 = attend(q, 0, masked)
        top1 = m_ref[q]
        top = jnp.maximum(top1, top2)
        f1 = jnp.exp2((top1 - top) * FACTOR)
        f2 = jnp.exp2((top2 - top) * FACTOR)
        whole = (f1 * acc_ref[q] + f2 * acc2) / (f1 * l_ref[q] + f2 * total2)
        whole = whole.astype(jnp.bfloat16)
        rows = pl.ds(pl.multiple_of(q * BLK, BLK), BLK)
        for h in range(QH):
            out_ref[rows, h * HD : (h + 1) * HD] = whole[h * BLK : (h + 1) * BLK]

    @pl.when(z >= 2)
    def _():
        vs_copy(1 - c).wait_recv()

        def gathered(q, _):
            second(q, False)
            return 0

        lax.fori_loop(0, 2, gathered, 0)

    @pl.when(z < 2)
    def _():
        load_part(0)

        def windowed(q, _):
            second(q, True)
            return 0

        lax.fori_loop(0, 2, windowed, 0)

    for kv in range(2):

        @pl.when(jnp.logical_not(here(z_target(kv))))
        def _():
            z_copy(kv).wait_send()

        for up in (False, True):

            @pl.when(f_live(up))
            def _():
                f_copy(kv, up).wait_send()

    for hi in range(3):
        for kv in range(2):
            for i in range(1, 4):

                @pl.when(p1_live(kv, hi, i))
                def _():
                    p1_copy(kv, hi, i).wait_send()

                if i == 2 and relayed(kv, hi):
                    continue

                @pl.when(p2_live(kv, hi, i))
                def _():
                    p2_copy(kv, hi, i).wait_send()

            for i in (1, 3) if relayed(kv, hi) else ():

                @pl.when(needed(hi, (row(kv) + 4 - i) % 4, x))
                def _():
                    far_copy(kv, hi, i).wait_send()

            for g in range(4):

                @pl.when(needed(hi, g, x))
                def _():
                    sib_copy(kv, hi, g).wait_send()

    @pl.when(z == 2)
    def _():
        for kv in range(2):
            for i in range(1, 4):
                vp_copy(kv, i).wait_send()
        vh_copy(1 - c).wait_send()
        for i in range(5):
            vz_copy(i).wait_send()

    @pl.when(z >= 2)
    def _():
        for i in range(1, 4):
            v1_copy(i).wait_send()
        for cc in range(2):

            @pl.when(c == cc)
            def _():
                for i in range(1, 4):
                    v2_copy(cc, i).wait_send()
                vs_copy(cc).wait_send()


def local_attention(queries, key_cache, value_cache, block_list, block_count):
    dma = pltpu.SemaphoreType.DMA
    rows = queries.shape[0] // 4
    return pl.pallas_call(
        attention_kernel,
        out_shape=jax.ShapeDtypeStruct((rows, QH * HD), jnp.bfloat16),
        in_specs=[
            pl.BlockSpec(memory_space=pl.ANY),
            pl.BlockSpec(memory_space=pl.ANY),
            pl.BlockSpec(memory_space=pl.ANY),
            pl.BlockSpec(memory_space=pl.ANY),
            pl.BlockSpec(memory_space=pl.ANY),
        ],
        out_specs=pl.BlockSpec(memory_space=pltpu.VMEM),
        scratch_shapes=[
            pltpu.SMEM((8, LIST), jnp.int32),
            pltpu.SMEM((8,), jnp.int32),
            pltpu.SMEM((8,), jnp.int32),
            pltpu.VMEM((2, 3, 4, 4, 2, 2, BLK, HD), jnp.bfloat16),
            pltpu.VMEM((2, 4, 4, BLK, HD), jnp.bfloat16),
            pltpu.VMEM((2 * BLK, QH * HD), jnp.bfloat16),
            pltpu.VMEM((2, PART * BLK, HD), jnp.bfloat16),
            pltpu.VMEM((2, PART * BLK, HD), jnp.bfloat16),
            pltpu.VMEM((QH * BLK, PART * BLK), jnp.float32),
            pltpu.VMEM((2, QH * BLK, HD), jnp.float32),
            pltpu.VMEM((2, QH * BLK, HD), jnp.float32),
            pltpu.VMEM((2, QH * BLK, HD), jnp.float32),
            pltpu.VMEM((2, 4, BLK, HD), jnp.bfloat16),
            pltpu.VMEM((2, 3, BLK, HD), jnp.bfloat16),
            pltpu.VMEM((2, BLK, HD), jnp.bfloat16),
            pltpu.VMEM((BLK, HD), jnp.bfloat16),
            dma((3,)),
            dma((2,)), dma((2, 3)), dma((2, 2)),
            dma((2, 3, 3)), dma((2, 3, 3)),
            dma((2, 3, 3)), dma((2, 3, 3)),
            dma((2, 3, 2)), dma((2, 3, 2)),
            dma((2, 3, 4)), dma((2, 3, 4)),
            dma((2, 3)), dma((2, 3)),
            dma, dma,
            dma((5,)), dma,
            dma((3,)), dma((3,)),
            dma((3,)), dma((3,)),
            dma, dma,
        ],
        compiler_params=pltpu.CompilerParams(collective_id=0, has_side_effects=True, vmem_limit_bytes=60 * 1024 * 1024),
    )(block_list, block_count, queries, key_cache.reshape(2, BLK, HD), value_cache.reshape(2, BLK, HD))


def solution(mesh):
    placed = (P("pb", None), P(("ka", "pb"), None), P(("ka", "pb"), None), P("pb", None), P("pb"))
    return jax.shard_map(
        local_attention, mesh=mesh, in_specs=placed, out_specs=P(("pb", "ka"), None), check_vma=False
    )
```

```python
import functools
import math

import jax
import jax.numpy as jnp
from jax import lax
from jax.experimental import pallas as pl
from jax.experimental.pallas import tpu as pltpu
from jax.sharding import PartitionSpec as P

HD = 128
QH = 4
BLK = 128
LIST = 32
NV = 16
PART = 16
CHUNK = 4
MASKED = -1e30
FACTOR = math.log2(math.e) / math.sqrt(HD)


def attention_kernel(
    list_hbm, count_hbm, q_hbm, k_hbm, v_hbm, out_ref,
    list_ref, count_ref, pick_ref,
    buf, vbuf, qs, kc, vc, s_ref, acc_ref, m_ref, part_out, part_in, half_out, half_in,
    in_sem, z_send, z_recv, f_send, p1_send, p1_recv, p2_send, p2_recv, f2_send, f2_recv, sib_send, sib_recv,
    vp_send, vp_recv, vh_send, vh_recv, vz_send, vz_recv, v1_send, v1_recv, v2_send, v2_recv, vs_send, vs_recv,
):
    p = lax.axis_index("pb")
    y = lax.axis_index("ka")
    z = p // 8
    x = (p // 2) % 4
    c = p % 2

    def dev(zz, xx, cc, yy):
        return (zz * 8 + xx * 2 + cc, yy)

    def remote(src, dst, ssem, rsem, device):
        return pltpu.make_async_remote_copy(
            src_ref=src, dst_ref=dst, send_sem=ssem, recv_sem=rsem,
            device_id=device, device_id_type=pl.DeviceIdType.MESH,
        )

    def have(hi):
        return z >= 2 - hi

    def needed(hi, g, xx):
        if hi == 1:
            return have(hi)
        if hi == 0:
            return have(hi) & (g >= xx)
        return g <= xx

    inputs = [
        pltpu.make_async_copy(list_hbm, list_ref, in_sem.at[0]),
        pltpu.make_async_copy(count_hbm, count_ref, in_sem.at[1]),
        pltpu.make_async_copy(q_hbm.at[pl.ds(pl.multiple_of(y * 256, 256), 256)], qs, in_sem.at[2]),
    ]
    for copy in inputs:
        copy.start()

    src = (k_hbm, v_hbm)
    g_own = z % 4
    half = 2 * y + z // 4
    z_plane = jnp.minimum(half + 1, 7)
    z_half = jnp.where(half == 7, 2, 1)

    def z_target(kv):
        xd, yd = (x, g_own) if kv == 0 else (g_own, x)
        return z_plane, xd, c, yd

    def z_source(kv, h):
        return (4 * (h % 2) + y, x, c, h // 2) if kv == 0 else (4 * (h % 2) + x, y, c, h // 2)

    def here(device):
        zz, xx, _, yy = device
        return (zz == z) & (xx == x) & (yy == y)

    barrier = pltpu.get_barrier_semaphore()
    partners = []
    always = z >= 0
    for i in range(1, 4):
        partners.append((always, (z, (x + i) % 4, c, y)))
        partners.append((always, (z, x, c, (y + i) % 4)))
    partners.append((always, (z, x, 1 - c, y)))
    partners.append((z >= 1, (jnp.maximum(z - 1, 0), x, c, y)))
    partners.append((z <= 6, (jnp.minimum(z + 1, 7), x, c, y)))
    for i in range(5):
        partners.append((z == 2, (3 + i, x, c, y)))
    partners.append((z >= 3, (2, x, c, y)))
    for kv in range(2):
        there = z_target(kv)
        partners.append((jnp.logical_not(here(there)), there))
        there = z_source(kv, jnp.maximum(z - 1, 0))
        partners.append(((z >= 1) & jnp.logical_not(here(there)), there))
        there = z_source(kv, 7)
        partners.append(((z == 7) & jnp.logical_not(here(there)), there))
    expected = jnp.int32(0)
    for live, there in partners:

        @pl.when(live)
        def _():
            pl.semaphore_signal(barrier, inc=1, device_id=dev(*there), device_id_type=pl.DeviceIdType.MESH)

        expected = expected + jnp.where(live, 1, 0)
    pl.semaphore_wait(barrier, expected)

    def z_copy(kv):
        region = buf.at[kv, z_half, g_own, x, c]
        return remote(src[kv], region, z_send.at[kv], z_recv.at[kv, z_half], dev(*z_target(kv)))

    for kv in range(2):
        own = here(z_target(kv))

        @pl.when(jnp.logical_not(own))
        def _():
            z_copy(kv).start()

        @pl.when(own)
        def _():
            pltpu.make_async_copy(src[kv], buf.at[kv, z_half, g_own, x, c], z_recv.at[kv, z_half]).start()

    def row(kv):
        return y if kv == 0 else x

    def col(kv):
        return x if kv == 0 else y

    def along(kv, i):
        return dev(z, (x + i) % 4, c, y) if kv == 0 else dev(z, x, c, (y + i) % 4)

    def across(kv, i):
        return dev(z, x, c, (y + i) % 4) if kv == 0 else dev(z, (x + i) % 4, c, y)

    sibling = dev(z, x, 1 - c, y)

    def p1_copy(kv, hi, i):
        region = buf.at[kv, hi, row(kv), col(kv), c]
        return remote(region, region, p1_send.at[kv, hi, i - 1], p1_recv.at[kv, hi, i - 1], along(kv, i))

    def p1_live(kv, hi, i):
        if kv == 1:
            return have(hi)
        wanted = needed(hi, y, (x + i) % 4)
        return wanted | (z == 2) if hi == 0 else wanted

    def p1_got(kv, hi):
        if kv == 1:
            return have(hi)
        wanted = needed(hi, y, x)
        return wanted | (z == 2) if hi == 0 else wanted

    def p2_copy(kv, hi, i):
        region = buf.at[kv, hi, row(kv), :, c]
        return remote(region, region, p2_send.at[kv, hi, i - 1], p2_recv.at[kv, hi, i - 1], across(kv, i))

    def relayed(kv, hi):
        return kv == 0 or hi == 1

    def far_copy(kv, hi, i):
        g, first = (row(kv) + 4 - i) % 4, 0 if i == 1 else 2
        region = buf.at[kv, hi, g, first : first + 2, c]
        return remote(region, region, f2_send.at[kv, hi, i // 2], f2_recv.at[kv, hi, i // 2], across(kv, i))

    def p2_live(kv, hi, i):
        return needed(hi, y, x) if kv == 0 else needed(hi, x, (x + i) % 4)

    def sib_copy(kv, hi, g):
        region = buf.at[kv, hi, g, :, c]
        return remote(region, region, sib_send.at[kv, hi, g], sib_recv.at[kv, hi, g], sibling)

    def vz_copy(i):
        return remote(vbuf.at[c, x, y], vbuf.at[c, x, y], vz_send.at[i], vz_recv, dev(3 + i, x, c, y))

    def v_line(first, i):
        to_x = (c == 0) == first
        return dev(z, jnp.where(to_x, (x + i) % 4, x), c, jnp.where(to_x, y, (y + i) % 4))

    def v1_copy(i):
        return remote(vbuf.at[c, x, y], vbuf.at[c, x, y], v1_send.at[i - 1], v1_recv.at[i - 1], v_line(True, i))

    def v2_copy(cc, i):
        region = vbuf.at[0, :, y] if cc == 0 else vbuf.at[1, x]
        return remote(region, region, v2_send.at[i - 1], v2_recv.at[i - 1], v_line(False, i))

    def vs_copy(cc):
        return remote(vbuf.at[cc], vbuf.at[cc], vs_send, vs_recv, sibling)

    def f_copy(kv, up):
        region = buf.at[kv, 1, row(kv), col(kv), c]
        there = buf.at[kv, 0 if up else 2, row(kv), col(kv), c]
        to = jnp.minimum(z + 1, 7) if up else jnp.maximum(z - 1, 0)
        return remote(region, there, f_send.at[kv, int(up)], z_recv.at[kv, 0 if up else 2], dev(to, x, c, y))

    def f_live(up):
        return (z >= 1) & (z <= 6) if up else z >= 1

    for copy in inputs[:2]:
        copy.wait()

    @pl.when(z == 2)
    def _():
        entries = [list_ref[2 * y, i] for i in range(NV)]
        slots = [4 * x + (y + i) % 4 for i in range(4)] + [4 * ((x + i) % 4) + y for i in range(4)]
        chosen = [jnp.int32(-1)] * 8
        for i in range(NV):
            rank = jnp.int32(0)
            for j in range(NV):
                if j != i:
                    rank = rank + jnp.where(entries[j] < entries[i], 1, 0)
            chosen = [jnp.where(rank == slot, entries[i], now) for slot, now in zip(slots, chosen)]
        for n in range(8):
            pick_ref[n] = chosen[n]

    for hi in (1, 0, 2):
        for kv in range(2):

            @pl.when(have(hi))
            def _():
                pltpu.make_async_copy(src[kv], buf.at[kv, hi, row(kv), col(kv), c], z_recv.at[kv, hi]).wait()

            if hi == 1:
                for up in (False, True):

                    @pl.when(f_live(up))
                    def _():
                        f_copy(kv, up).start()

            for i in (1, 3, 2):

                @pl.when(p1_live(kv, hi, i))
                def _():
                    p1_copy(kv, hi, i).start()

    def p1_wait(hi):
        for kv in range(2):
            for i in (1, 3, 2):

                @pl.when(p1_got(kv, hi))
                def _():
                    region = buf.at[kv, hi, row(kv), (col(kv) + 4 - i) % 4, c]
                    remote(region, region, p1_send.at[kv, hi, i - 1], p1_recv.at[kv, hi, i - 1], sibling).wait_recv()

    def p2_start(hi, when):
        for kv in range(2):
            for i in (1, 3) if relayed(kv, hi) else (1, 3, 2):

                @pl.when(p2_live(kv, hi, i) & when)
                def _():
                    p2_copy(kv, hi, i).start()

            @pl.when(needed(hi, row(kv), x) & when)
            def _():
                sib_copy(kv, hi, row(kv)).start()

    def near(hi):
        for i in (1, 3):
            for kv in range(2):
                g = (row(kv) + 4 - i) % 4

                @pl.when(needed(hi, g, x))
                def _():
                    region = buf.at[kv, hi, g, :, c]
                    remote(region, region, p2_send.at[kv, hi, i - 1], p2_recv.at[kv, hi, i - 1], sibling).wait_recv()
                    if relayed(kv, hi):
                        far_copy(kv, hi, i).start()
                    sib_copy(kv, hi, g).start()

    def far(hi):
        for kv in range(2):
            g = (row(kv) + 2) % 4

            @pl.when(needed(hi, g, x))
            def _():
                if relayed(kv, hi):
                    for i in (1, 3):
                        first = 0 if i == 1 else 2
                        region = buf.at[kv, hi, g, first : first + 2, c]
                        remote(region, region, f2_send.at[kv, hi, i // 2], f2_recv.at[kv, hi, i // 2], sibling).wait_recv()
                else:
                    region = buf.at[kv, hi, g, :, c]
                    remote(region, region, p2_send.at[kv, hi, 1], p2_recv.at[kv, hi, 1], sibling).wait_recv()
                sib_copy(kv, hi, g).start()

    def vp_copy(kv, i):
        return remote(
            part_out.at[kv, i], part_in.at[kv, i - 1], vp_send.at[kv, i - 1], vp_recv.at[kv, i - 1], across(kv, i)
        )

    def vh_copy(kv):
        return remote(half_out.at[kv], half_in, vh_send, vh_recv, sibling)

    p1_wait(1)
    p2_start(1, z >= 0)
    p1_wait(0)

    @pl.when(z == 2)
    def _():
        for kv in range(2):

            picked = [jnp.zeros((BLK, HD), jnp.bfloat16)] * 4
            for hi in range(2):
                for l in range(4):
                    for r in range(2):
                        block = buf[kv, hi, row(kv), l, c, r]
                        name = 64 * hi + 16 * row(kv) + 4 * l + 2 * c + r
                        picked = [jnp.where(pick_ref[4 * kv + i] == name, block, picked[i]) for i in range(4)]
            for i in range(4):
                part_out[kv, i] = picked[i]
            for i in (1, 3, 2):
                vp_copy(kv, i).start()

    p2_start(0, z >= 0)
    p1_wait(2)
    p2_start(2, z >= 0)

    @pl.when(z == 2)
    def _():
        for kv in range(2):
            for i in (1, 3, 2):
                vp_copy(kv, i).wait_recv()
            half_out[kv] = (part_out[kv, 0] + part_in[kv, 0]) + (part_in[kv, 1] + part_in[kv, 2])
        vh_copy(1 - c).start()
        vh_copy(c).wait_recv()
        vbuf[c, x, y] = half_out[c] + half_in[...]
        for i in (0, 4, 1, 3, 2):
            vz_copy(i).start()

    near(1)
    near(0)

    @pl.when(z >= 3)
    def _():
        vz_copy(0).wait_recv()

    @pl.when(z >= 2)
    def _():
        for i in (1, 3, 2):
            v1_copy(i).start()

    far(1)
    near(2)

    @pl.when(z >= 2)
    def _():
        for i in (1, 3, 2):
            v1_copy(i).wait_recv()
        for cc in range(2):

            @pl.when(c == cc)
            def _():
                for i in (1, 3, 2):
                    v2_copy(cc, i).start()

    far(0)
    far(2)
    for hi in (1, 0, 2):
        for kv in range(2):
            for g in range(4):

                @pl.when(needed(hi, g, x))
                def _():
                    region = buf.at[kv, hi, g, :, 1 - c]
                    remote(region, region, sib_send.at[kv, hi, g], sib_recv.at[kv, hi, g], sibling).wait_recv()

    def place(block):
        rel = jnp.clip(block - 64 * (z - 2), 0, 191)
        return rel >> 6, (rel >> 4) & 3, (rel >> 2) & 3, (rel >> 1) & 1, rel & 1

    def block_of(kv, block):
        hi, g, l, cc, r = place(block)
        return buf[kv, hi, g, l, cc, r]

    delta = lax.broadcasted_iota(jnp.int32, (BLK, BLK), 1) - lax.broadcasted_iota(jnp.int32, (BLK, BLK), 0)

    ones = jnp.ones((CHUNK * BLK, HD), jnp.bfloat16)
    second_set = jnp.where(z >= 2, 0, 1)

    def keys_of(kv, q, part, n):
        if part == 1:
            return jnp.concatenate(
                [block_of(kv, list_ref[2 * y + q, PART + n * CHUNK + k]) for k in range(CHUNK)], axis=0
            )
        held = kc if kv == 0 else vc
        return held[q * second_set, n * CHUNK * BLK : (n + 1) * CHUNK * BLK, :]

    queries_of = []

    def score_chunk(q, part, n, peak):
        my_block = 8 * p + 2 * y + q
        count = count_ref[2 * y + q]
        scores = lax.dot_general(
            queries_of[q], keys_of(0, q, part, n), (((1,), (1,)), ((), ())), preferred_element_type=jnp.float32
        )
        for k in range(CHUNK):
            slot = part * PART + n * CHUNK + k
            block = list_ref[2 * y + q, slot]
            reach = jnp.where(block == my_block, 0, BLK)
            reach = jnp.where(slot < count, reach, -BLK)
            ok = delta <= reach
            tile = scores[:, k * BLK : (k + 1) * BLK].reshape(QH, BLK, BLK)
            tile = jnp.where(ok[None], tile, MASKED).reshape(QH * BLK, BLK)
            s_ref[q, :, (n * CHUNK + k) * BLK : (n * CHUNK + k + 1) * BLK] = tile
            peak = tile if peak is None else jnp.maximum(peak, tile)
        return peak

    def apply_chunk(q, part, n, top, acc):
        scores = s_ref[q, :, n * CHUNK * BLK : (n + 1) * CHUNK * BLK]
        weights = jnp.exp2((scores - top) * FACTOR).astype(jnp.bfloat16)
        values = jnp.concatenate([keys_of(1, q, part, n), ones], axis=1)
        out = jnp.dot(weights, values, preferred_element_type=jnp.float32)
        return out if acc is None else acc + out

    def stage(scored, applied, top):
        peak = acc = None
        for n in range(PART // CHUNK):
            if scored is not None:
                peak = score_chunk(*scored, n, peak)
            if applied is not None:
                acc = apply_chunk(*applied, n, top, acc)
        next_top = None if peak is None else jnp.max(peak, axis=1, keepdims=True)
        return next_top, acc

    def keep(q, top, acc):
        acc_ref[q] = acc
        m_ref[q] = jnp.broadcast_to(top, (QH * BLK, HD))

    def finish(q, top2, acc2):
        top1 = m_ref[q]
        top = jnp.maximum(top1, top2)
        f1 = jnp.exp2((top1 - top) * FACTOR)
        f2 = jnp.exp2((top2 - top) * FACTOR)
        total = f1 * acc_ref[q, :, HD:] + f2 * acc2[:, HD:]
        whole = ((f1 * acc_ref[q, :, :HD] + f2 * acc2[:, :HD]) / total).astype(jnp.bfloat16)
        for h in range(QH):
            out_ref[q * BLK : (q + 1) * BLK, h * HD : (h + 1) * HD] = whole[h * BLK : (h + 1) * BLK]

    inputs[2].wait()
    for q in range(2):
        queries_of.append(
            jnp.concatenate([qs[q * BLK : (q + 1) * BLK, h * HD : (h + 1) * HD] for h in range(QH)], axis=0)
        )

    @pl.when(z < 2)
    def _():
        def load(n, _):
            q = n // PART
            s = n % PART
            block = list_ref[2 * y + q, s]
            rows = pl.ds(pl.multiple_of(s * BLK, BLK), BLK)
            kc[q, rows, :] = block_of(0, block)
            vc[q, rows, :] = block_of(1, block)
            return 0

        lax.fori_loop(0, 2 * PART, load, 0)

    top_s0, _ = stage((0, 1), None, None)

    @pl.when(z >= 2)
    def _():
        for cc in range(2):

            @pl.when(c == cc)
            def _():
                for i in (1, 3, 2):
                    v2_copy(cc, i).wait_recv()
                vs_copy(cc).start()

    top_s1, acc_s0 = stage((1, 1), (0, 1), top_s0)
    keep(0, top_s0, acc_s0)

    @pl.when(z >= 2)
    def _():
        vs_copy(1 - c).wait_recv()
        kc[0] = vbuf[0].reshape(PART * BLK, HD)
        vc[0] = vbuf[1].reshape(PART * BLK, HD)

    top_v0, acc_s1 = stage((0, 0), (1, 1), top_s1)
    keep(1, top_s1, acc_s1)
    top_v1, acc_v0 = stage((1, 0), (0, 0), top_v0)
    finish(0, top_v0, acc_v0)
    _, acc_v1 = stage(None, (1, 0), top_v1)
    finish(1, top_v1, acc_v1)

    for kv in range(2):

        @pl.when(jnp.logical_not(here(z_target(kv))))
        def _():
            z_copy(kv).wait_send()

        for up in (False, True):

            @pl.when(f_live(up))
            def _():
                f_copy(kv, up).wait_send()

    for hi in range(3):
        for kv in range(2):
            for i in range(1, 4):

                @pl.when(p1_live(kv, hi, i))
                def _():
                    p1_copy(kv, hi, i).wait_send()

                if i == 2 and relayed(kv, hi):
                    continue

                @pl.when(p2_live(kv, hi, i))
                def _():
                    p2_copy(kv, hi, i).wait_send()

            for i in (1, 3) if relayed(kv, hi) else ():

                @pl.when(needed(hi, (row(kv) + 4 - i) % 4, x))
                def _():
                    far_copy(kv, hi, i).wait_send()

            for g in range(4):

                @pl.when(needed(hi, g, x))
                def _():
                    sib_copy(kv, hi, g).wait_send()

    @pl.when(z == 2)
    def _():
        for kv in range(2):
            for i in range(1, 4):
                vp_copy(kv, i).wait_send()
        vh_copy(1 - c).wait_send()
        for i in range(5):
            vz_copy(i).wait_send()

    @pl.when(z >= 2)
    def _():
        for i in range(1, 4):
            v1_copy(i).wait_send()
        for cc in range(2):

            @pl.when(c == cc)
            def _():
                for i in range(1, 4):
                    v2_copy(cc, i).wait_send()
                vs_copy(cc).wait_send()


def local_attention(queries, key_cache, value_cache, block_list, block_count):
    dma = pltpu.SemaphoreType.DMA
    rows = queries.shape[0] // 4
    return pl.pallas_call(
        attention_kernel,
        out_shape=jax.ShapeDtypeStruct((rows, QH * HD), jnp.bfloat16),
        in_specs=[
            pl.BlockSpec(memory_space=pl.ANY),
            pl.BlockSpec(memory_space=pl.ANY),
            pl.BlockSpec(memory_space=pl.ANY),
            pl.BlockSpec(memory_space=pl.ANY),
            pl.BlockSpec(memory_space=pl.ANY),
        ],
        out_specs=pl.BlockSpec(memory_space=pltpu.VMEM),
        scratch_shapes=[
            pltpu.SMEM((8, LIST), jnp.int32),
            pltpu.SMEM((8,), jnp.int32),
            pltpu.SMEM((8,), jnp.int32),
            pltpu.VMEM((2, 3, 4, 4, 2, 2, BLK, HD), jnp.bfloat16),
            pltpu.VMEM((2, 4, 4, BLK, HD), jnp.bfloat16),
            pltpu.VMEM((2 * BLK, QH * HD), jnp.bfloat16),
            pltpu.VMEM((2, PART * BLK, HD), jnp.bfloat16),
            pltpu.VMEM((2, PART * BLK, HD), jnp.bfloat16),
            pltpu.VMEM((2, QH * BLK, PART * BLK), jnp.float32),
            pltpu.VMEM((2, QH * BLK, 2 * HD), jnp.float32),
            pltpu.VMEM((2, QH * BLK, HD), jnp.float32),
            pltpu.VMEM((2, 4, BLK, HD), jnp.bfloat16),
            pltpu.VMEM((2, 3, BLK, HD), jnp.bfloat16),
            pltpu.VMEM((2, BLK, HD), jnp.bfloat16),
            pltpu.VMEM((BLK, HD), jnp.bfloat16),
            dma((3,)),
            dma((2,)), dma((2, 3)), dma((2, 2)),
            dma((2, 3, 3)), dma((2, 3, 3)),
            dma((2, 3, 3)), dma((2, 3, 3)),
            dma((2, 3, 2)), dma((2, 3, 2)),
            dma((2, 3, 4)), dma((2, 3, 4)),
            dma((2, 3)), dma((2, 3)),
            dma, dma,
            dma((5,)), dma,
            dma((3,)), dma((3,)),
            dma((3,)), dma((3,)),
            dma, dma,
        ],
        compiler_params=pltpu.CompilerParams(collective_id=0, has_side_effects=True, vmem_limit_bytes=60 * 1024 * 1024),
    )(block_list, block_count, queries, key_cache.reshape(2, BLK, HD), value_cache.reshape(2, BLK, HD))


def solution(mesh):
    placed = (P("pb", None), P(("ka", "pb"), None), P(("ka", "pb"), None), P("pb", None), P("pb"))
    return jax.shard_map(
        local_attention, mesh=mesh, in_specs=placed, out_specs=P(("pb", "ka"), None), check_vma=False
    )
```

```python
import functools
import math

import jax
import jax.numpy as jnp
from jax import lax
from jax.experimental import pallas as pl
from jax.experimental.pallas import tpu as pltpu
from jax.sharding import PartitionSpec as P

HD = 128
QH = 4
BLK = 128
LIST = 32
NV = 16
PART = 16
CHUNK = 4
MASKED = -1e30
FACTOR = math.log2(math.e) / math.sqrt(HD)


def attention_kernel(
    list_hbm, count_hbm, q_hbm, k_hbm, v_hbm, out_ref,
    list_ref, count_ref, pick_ref, told_ref, list_vm,
    k_win, v_win, vbuf, qs, kc, vc, s_ref, acc_ref, m_ref, part_out, part_in, half_out, half_in,
    in_sem, z_send, z_recv, f_send, p1_send, p1_recv, p2_send, p2_recv, f2_send, f2_recv, sib_send, sib_recv,
    vp_send, vp_recv, vh_send, vh_recv, vz_send, vz_recv, v1_send, v1_recv, v2_send, v2_recv, vs_send, vs_recv, tell_send, tell_recv,
):
    win = (k_win, v_win)
    p = lax.axis_index("pb")
    y = lax.axis_index("ka")
    z = p // 8
    x = (p // 2) % 4
    c = p % 2

    def dev(zz, xx, cc, yy):
        return (zz * 8 + xx * 2 + cc, yy)

    def remote(src, dst, ssem, rsem, device):
        return pltpu.make_async_remote_copy(
            src_ref=src, dst_ref=dst, send_sem=ssem, recv_sem=rsem,
            device_id=device, device_id_type=pl.DeviceIdType.MESH,
        )

    def have(hi):
        return z >= 2 - hi

    def needed(hi, g, xx):
        if hi == 1:
            return have(hi)
        if hi == 0:
            return have(hi) & (g >= xx)
        return g <= xx

    inputs = [
        pltpu.make_async_copy(list_hbm, list_ref, in_sem.at[0]),
        pltpu.make_async_copy(count_hbm, count_ref, in_sem.at[1]),
        pltpu.make_async_copy(q_hbm.at[pl.ds(pl.multiple_of(y * 256, 256), 256)], qs, in_sem.at[2]),
    ]
    for copy in inputs:
        copy.start()

    src = (k_hbm, v_hbm)
    g_own = z % 4
    half = 2 * y + z // 4
    z_plane = jnp.minimum(half + 1, 7)
    z_half = jnp.where(half == 7, 2, 1)

    def z_target(kv):
        xd, yd = (x, g_own) if kv == 0 else (g_own, x)
        return z_plane, xd, c, yd

    def z_source(kv, h):
        return (4 * (h % 2) + y, x, c, h // 2) if kv == 0 else (4 * (h % 2) + x, y, c, h // 2)

    def here(device):
        zz, xx, _, yy = device
        return (zz == z) & (xx == x) & (yy == y)

    barrier = pltpu.get_barrier_semaphore()
    partners = []
    always = z >= 0
    for i in range(1, 4):
        partners.append((always, (z, (x + i) % 4, c, y)))
        partners.append((always, (z, x, c, (y + i) % 4)))
    partners.append((always, (z, x, 1 - c, y)))
    partners.append((z >= 1, (jnp.maximum(z - 1, 0), x, c, y)))
    partners.append((z <= 6, (jnp.minimum(z + 1, 7), x, c, y)))
    for i in range(6):
        partners.append((z == 1, (2 + i, x, c, y)))
    partners.append((z >= 2, (1, x, c, y)))
    for kv in range(2):
        there = z_target(kv)
        partners.append((jnp.logical_not(here(there)), there))
        there = z_source(kv, jnp.maximum(z - 1, 0))
        partners.append(((z >= 1) & jnp.logical_not(here(there)), there))
        there = z_source(kv, 7)
        partners.append(((z == 7) & jnp.logical_not(here(there)), there))
    expected = jnp.int32(0)
    for live, there in partners:

        @pl.when(live)
        def _():
            pl.semaphore_signal(barrier, inc=1, device_id=dev(*there), device_id_type=pl.DeviceIdType.MESH)

        expected = expected + jnp.where(live, 1, 0)
    pl.semaphore_wait(barrier, expected)

    def z_copy(kv):
        region = win[kv].at[z_half, g_own, x, c]
        return remote(src[kv], region, z_send.at[kv], z_recv.at[kv, z_half], dev(*z_target(kv)))

    for kv in range(2):
        own = here(z_target(kv))

        @pl.when(jnp.logical_not(own))
        def _():
            z_copy(kv).start()

        @pl.when(own)
        def _():
            pltpu.make_async_copy(src[kv], win[kv].at[z_half, g_own, x, c], z_recv.at[kv, z_half]).start()

    def row(kv):
        return y if kv == 0 else x

    def col(kv):
        return x if kv == 0 else y

    def along(kv, i):
        return dev(z, (x + i) % 4, c, y) if kv == 0 else dev(z, x, c, (y + i) % 4)

    def across(kv, i):
        return dev(z, x, c, (y + i) % 4) if kv == 0 else dev(z, (x + i) % 4, c, y)

    sibling = dev(z, x, 1 - c, y)

    def p1_copy(kv, hi, i):
        region = win[kv].at[hi, row(kv), col(kv), c]
        return remote(region, region, p1_send.at[kv, hi, i - 1], p1_recv.at[kv, hi, i - 1], along(kv, i))

    def p1_live(kv, hi, i):
        if kv == 1:
            return have(hi)
        wanted = needed(hi, y, (x + i) % 4)
        return wanted | (z == 1) if hi == 2 else wanted

    def p1_got(kv, hi):
        if kv == 1:
            return have(hi)
        wanted = needed(hi, y, x)
        return wanted | (z == 1) if hi == 2 else wanted

    def p2_copy(kv, hi, i):
        region = win[kv].at[hi, row(kv), :, c]
        return remote(region, region, p2_send.at[kv, hi, i - 1], p2_recv.at[kv, hi, i - 1], across(kv, i))

    def relayed(kv, hi):
        return kv == 0 or hi == 1

    def far_copy(kv, hi, i):
        g, first = (row(kv) + 4 - i) % 4, 0 if i == 1 else 2
        region = win[kv].at[hi, g, first : first + 2, c]
        return remote(region, region, f2_send.at[kv, hi, i // 2], f2_recv.at[kv, hi, i // 2], across(kv, i))

    def p2_live(kv, hi, i):
        return needed(hi, y, x) if kv == 0 else needed(hi, x, (x + i) % 4)

    def sib_copy(kv, hi, g):
        region = win[kv].at[hi, g, :, c]
        return remote(region, region, sib_send.at[kv, hi, g], sib_recv.at[kv, hi, g], sibling)

    def vz_copy(i):
        return remote(vbuf.at[c, x, y], vbuf.at[c, x, y], vz_send.at[i], vz_recv, dev(2 + i, x, c, y))

    def v_line(first, i):
        to_x = (c == 0) == first
        return dev(z, jnp.where(to_x, (x + i) % 4, x), c, jnp.where(to_x, y, (y + i) % 4))

    def v1_copy(i):
        return remote(vbuf.at[c, x, y], vbuf.at[c, x, y], v1_send.at[i - 1], v1_recv.at[i - 1], v_line(True, i))

    def v2_copy(cc, i):
        region = vbuf.at[0, :, y] if cc == 0 else vbuf.at[1, x]
        return remote(region, region, v2_send.at[i - 1], v2_recv.at[i - 1], v_line(False, i))

    def vs_copy(cc):
        return remote(vbuf.at[cc], vbuf.at[cc], vs_send, vs_recv, sibling)

    def f_copy(kv, up):
        region = win[kv].at[1, row(kv), col(kv), c]
        there = win[kv].at[0 if up else 2, row(kv), col(kv), c]
        to = jnp.minimum(z + 1, 7) if up else jnp.maximum(z - 1, 0)
        return remote(region, there, f_send.at[kv, int(up)], z_recv.at[kv, 0 if up else 2], dev(to, x, c, y))

    def f_live(up):
        return (z >= 1) & (z <= 6) if up else z >= 1

    for copy in inputs[:2]:
        copy.wait()

    tell = remote(list_hbm, list_vm, tell_send, tell_recv, dev(1, x, c, y))

    @pl.when(z == 2)
    def _():
        tell.start()

    @pl.when(z == 1)
    def _():
        tell.wait_recv()
        told = pltpu.make_async_copy(list_vm, told_ref, in_sem.at[3])
        told.start()
        told.wait()
        entries = [told_ref[0, i] for i in range(NV)]
        slots = [4 * x + (y + i) % 4 for i in range(4)] + [4 * ((x + i) % 4) + y for i in range(4)]
        chosen = [jnp.int32(-1)] * 8
        for i in range(NV):
            rank = jnp.int32(0)
            for j in range(NV):
                if j != i:
                    rank = rank + jnp.where(entries[j] < entries[i], 1, 0)
            chosen = [jnp.where(rank == slot, entries[i], now) for slot, now in zip(slots, chosen)]
        for n in range(8):
            pick_ref[n] = chosen[n]

    for hi in (1, 0, 2):
        for kv in range(2):

            @pl.when(have(hi))
            def _():
                pltpu.make_async_copy(src[kv], win[kv].at[hi, row(kv), col(kv), c], z_recv.at[kv, hi]).wait()

            if hi == 1:
                for up in (False, True):

                    @pl.when(f_live(up))
                    def _():
                        f_copy(kv, up).start()

            for i in (1, 3, 2):

                @pl.when(p1_live(kv, hi, i))
                def _():
                    p1_copy(kv, hi, i).start()

    def p1_wait(hi):
        for kv in range(2):
            for i in (1, 3, 2):

                @pl.when(p1_got(kv, hi))
                def _():
                    region = win[kv].at[hi, row(kv), (col(kv) + 4 - i) % 4, c]
                    remote(region, region, p1_send.at[kv, hi, i - 1], p1_recv.at[kv, hi, i - 1], sibling).wait_recv()

    def p2_start(hi, when):
        for kv in range(2):
            for i in (1, 3) if relayed(kv, hi) else (1, 3, 2):

                @pl.when(p2_live(kv, hi, i) & when)
                def _():
                    p2_copy(kv, hi, i).start()

            @pl.when(needed(hi, row(kv), x) & when)
            def _():
                sib_copy(kv, hi, row(kv)).start()

    def near(hi):
        for i in (1, 3):
            for kv in range(2):
                g = (row(kv) + 4 - i) % 4

                @pl.when(needed(hi, g, x))
                def _():
                    region = win[kv].at[hi, g, :, c]
                    remote(region, region, p2_send.at[kv, hi, i - 1], p2_recv.at[kv, hi, i - 1], sibling).wait_recv()
                    if relayed(kv, hi):
                        far_copy(kv, hi, i).start()
                    sib_copy(kv, hi, g).start()

    def far(hi, kvs=(0, 1)):
        for kv in kvs:
            g = (row(kv) + 2) % 4

            @pl.when(needed(hi, g, x))
            def _():
                if relayed(kv, hi):
                    for i in (1, 3):
                        first = 0 if i == 1 else 2
                        region = win[kv].at[hi, g, first : first + 2, c]
                        remote(region, region, f2_send.at[kv, hi, i // 2], f2_recv.at[kv, hi, i // 2], sibling).wait_recv()
                else:
                    region = win[kv].at[hi, g, :, c]
                    remote(region, region, p2_send.at[kv, hi, 1], p2_recv.at[kv, hi, 1], sibling).wait_recv()
                sib_copy(kv, hi, g).start()

    def vp_copy(kv, i):
        return remote(
            part_out.at[kv, i], part_in.at[kv, i - 1], vp_send.at[kv, i - 1], vp_recv.at[kv, i - 1], across(kv, i)
        )

    def vh_copy(kv):
        return remote(half_out.at[kv], half_in, vh_send, vh_recv, sibling)

    p1_wait(1)
    p2_start(1, z != 1)
    p1_wait(0)
    p2_start(0, z >= 0)
    p1_wait(2)

    @pl.when(z == 1)
    def _():
        for kv in range(2):

            picked = [jnp.zeros((BLK, HD), jnp.bfloat16)] * 4
            for half_name in range(2):
                for l in range(4):
                    for r in range(2):
                        block = win[kv][1 + half_name, row(kv), l, c, r]
                        name = 64 * half_name + 16 * row(kv) + 4 * l + 2 * c + r
                        picked = [jnp.where(pick_ref[4 * kv + i] == name, block, picked[i]) for i in range(4)]
            for i in range(4):
                part_out[kv, i] = picked[i]
            for i in (1, 3, 2):
                vp_copy(kv, i).start()

    p2_start(1, z == 1)
    p2_start(2, z >= 0)

    @pl.when(z == 1)
    def _():
        for kv in range(2):
            for i in (1, 3, 2):
                vp_copy(kv, i).wait_recv()
            half_out[kv] = (part_out[kv, 0] + part_in[kv, 0]) + (part_in[kv, 1] + part_in[kv, 2])
        vh_copy(1 - c).start()
        vh_copy(c).wait_recv()
        vbuf[c, x, y] = half_out[c] + half_in[...]
        for i in (0, 5, 1, 4, 2, 3):
            vz_copy(i).start()

    near(1)
    near(0)

    @pl.when(z >= 2)
    def _():
        vz_copy(0).wait_recv()

    @pl.when(z >= 2)
    def _():
        for i in (1, 3, 2):
            v1_copy(i).start()

    far(1)
    near(2)

    @pl.when(z >= 2)
    def _():
        for i in (1, 3, 2):
            v1_copy(i).wait_recv()
        for cc in range(2):

            @pl.when(c == cc)
            def _():
                for i in (1, 3, 2):
                    v2_copy(cc, i).start()

    far(0)
    far(2)
    def window_wait(kv):
        for hi in (1, 0, 2):
            for g in range(4):

                @pl.when(needed(hi, g, x))
                def _():
                    region = win[kv].at[hi, g, :, 1 - c]
                    remote(region, region, sib_send.at[kv, hi, g], sib_recv.at[kv, hi, g], sibling).wait_recv()

    def place(block):
        rel = jnp.clip(block - 64 * (z - 2), 0, 191)
        return rel >> 6, (rel >> 4) & 3, (rel >> 2) & 3, (rel >> 1) & 1, rel & 1

    def block_of(kv, block):
        hi, g, l, cc, r = place(block)
        return win[kv][hi, g, l, cc, r]

    delta = lax.broadcasted_iota(jnp.int32, (BLK, BLK), 1) - lax.broadcasted_iota(jnp.int32, (BLK, BLK), 0)

    ones = jnp.ones((CHUNK * BLK, HD), jnp.bfloat16)
    second_set = jnp.where(z >= 2, 0, 1)

    def keys_of(kv, q, part, n):
        if part == 1:
            return jnp.concatenate(
                [block_of(kv, list_ref[2 * y + q, PART + n * CHUNK + k]) for k in range(CHUNK)], axis=0
            )
        held = kc if kv == 0 else vc
        return held[q * second_set, n * CHUNK * BLK : (n + 1) * CHUNK * BLK, :]

    queries_of = []

    def score_chunk(q, part, n, peak):
        my_block = 8 * p + 2 * y + q
        count = count_ref[2 * y + q]
        scores = lax.dot_general(
            queries_of[q], keys_of(0, q, part, n), (((1,), (1,)), ((), ())), preferred_element_type=jnp.float32
        )
        for k in range(CHUNK):
            slot = part * PART + n * CHUNK + k
            block = list_ref[2 * y + q, slot]
            reach = jnp.where(block == my_block, 0, BLK)
            reach = jnp.where(slot < count, reach, -BLK)
            ok = delta <= reach
            tile = scores[:, k * BLK : (k + 1) * BLK].reshape(QH, BLK, BLK)
            tile = jnp.where(ok[None], tile, MASKED).reshape(QH * BLK, BLK)
            s_ref[q, :, (n * CHUNK + k) * BLK : (n * CHUNK + k + 1) * BLK] = tile
            peak = tile if peak is None else jnp.maximum(peak, tile)
        return peak

    def apply_chunk(q, part, n, top, acc):
        scores = s_ref[q, :, n * CHUNK * BLK : (n + 1) * CHUNK * BLK]
        weights = jnp.exp2((scores - top) * FACTOR).astype(jnp.bfloat16)
        values = jnp.concatenate([keys_of(1, q, part, n), ones], axis=1)
        out = jnp.dot(weights, values, preferred_element_type=jnp.float32)
        return out if acc is None else acc + out

    def stage(scored, applied, top):
        peak = acc = None
        for n in range(PART // CHUNK):
            if scored is not None:
                peak = score_chunk(*scored, n, peak)
            if applied is not None:
                acc = apply_chunk(*applied, n, top, acc)
        next_top = None if peak is None else jnp.max(peak, axis=1, keepdims=True)
        return next_top, acc

    def keep(q, top, acc):
        acc_ref[q] = acc
        m_ref[q] = jnp.broadcast_to(top, (QH * BLK, HD))

    def finish(q, top2, acc2):
        top1 = m_ref[q]
        top = jnp.maximum(top1, top2)
        f1 = jnp.exp2((top1 - top) * FACTOR)
        f2 = jnp.exp2((top2 - top) * FACTOR)
        total = f1 * acc_ref[q, :, HD:] + f2 * acc2[:, HD:]
        whole = ((f1 * acc_ref[q, :, :HD] + f2 * acc2[:, :HD]) / total).astype(jnp.bfloat16)
        for h in range(QH):
            out_ref[q * BLK : (q + 1) * BLK, h * HD : (h + 1) * HD] = whole[h * BLK : (h + 1) * BLK]

    inputs[2].wait()
    for q in range(2):
        queries_of.append(
            jnp.concatenate([qs[q * BLK : (q + 1) * BLK, h * HD : (h + 1) * HD] for h in range(QH)], axis=0)
        )

    window_wait(0)
    top_s0, _ = stage((0, 1), None, None)
    window_wait(1)

    @pl.when(z < 2)
    def _():
        def load(n, _):
            q = n // PART
            s = n % PART
            block = list_ref[2 * y + q, s]
            rows = pl.ds(pl.multiple_of(s * BLK, BLK), BLK)
            kc[q, rows, :] = block_of(0, block)
            vc[q, rows, :] = block_of(1, block)
            return 0

        lax.fori_loop(0, 2 * PART, load, 0)

    @pl.when(z >= 2)
    def _():
        for cc in range(2):

            @pl.when(c == cc)
            def _():
                for i in (1, 3, 2):
                    v2_copy(cc, i).wait_recv()
                vs_copy(cc).start()

    top_s1, acc_s0 = stage((1, 1), (0, 1), top_s0)
    keep(0, top_s0, acc_s0)

    @pl.when(z >= 2)
    def _():
        vs_copy(1 - c).wait_recv()
        kc[0] = vbuf[0].reshape(PART * BLK, HD)
        vc[0] = vbuf[1].reshape(PART * BLK, HD)

    top_v0, acc_s1 = stage((0, 0), (1, 1), top_s1)
    keep(1, top_s1, acc_s1)
    top_v1, acc_v0 = stage((1, 0), (0, 0), top_v0)
    finish(0, top_v0, acc_v0)
    _, acc_v1 = stage(None, (1, 0), top_v1)
    finish(1, top_v1, acc_v1)

    for kv in range(2):

        @pl.when(jnp.logical_not(here(z_target(kv))))
        def _():
            z_copy(kv).wait_send()

        for up in (False, True):

            @pl.when(f_live(up))
            def _():
                f_copy(kv, up).wait_send()

    for hi in range(3):
        for kv in range(2):
            for i in range(1, 4):

                @pl.when(p1_live(kv, hi, i))
                def _():
                    p1_copy(kv, hi, i).wait_send()

                if i == 2 and relayed(kv, hi):
                    continue

                @pl.when(p2_live(kv, hi, i))
                def _():
                    p2_copy(kv, hi, i).wait_send()

            for i in (1, 3) if relayed(kv, hi) else ():

                @pl.when(needed(hi, (row(kv) + 4 - i) % 4, x))
                def _():
                    far_copy(kv, hi, i).wait_send()

            for g in range(4):

                @pl.when(needed(hi, g, x))
                def _():
                    sib_copy(kv, hi, g).wait_send()

    @pl.when(z == 2)
    def _():
        tell.wait_send()

    @pl.when(z == 1)
    def _():
        for kv in range(2):
            for i in range(1, 4):
                vp_copy(kv, i).wait_send()
        vh_copy(1 - c).wait_send()
        for i in range(6):
            vz_copy(i).wait_send()

    @pl.when(z >= 2)
    def _():
        for i in range(1, 4):
            v1_copy(i).wait_send()
        for cc in range(2):

            @pl.when(c == cc)
            def _():
                for i in range(1, 4):
                    v2_copy(cc, i).wait_send()
                vs_copy(cc).wait_send()


def local_attention(queries, key_cache, value_cache, block_list, block_count):
    dma = pltpu.SemaphoreType.DMA
    rows = queries.shape[0] // 4
    return pl.pallas_call(
        attention_kernel,
        out_shape=jax.ShapeDtypeStruct((rows, QH * HD), jnp.bfloat16),
        in_specs=[
            pl.BlockSpec(memory_space=pl.ANY),
            pl.BlockSpec(memory_space=pl.ANY),
            pl.BlockSpec(memory_space=pl.ANY),
            pl.BlockSpec(memory_space=pl.ANY),
            pl.BlockSpec(memory_space=pl.ANY),
        ],
        out_specs=pl.BlockSpec(memory_space=pltpu.VMEM),
        scratch_shapes=[
            pltpu.SMEM((8, LIST), jnp.int32),
            pltpu.SMEM((8,), jnp.int32),
            pltpu.SMEM((8,), jnp.int32),
            pltpu.SMEM((8, LIST), jnp.int32),
            pltpu.VMEM((8, LIST), jnp.int32),
            pltpu.VMEM((3, 4, 4, 2, 2, BLK, HD), jnp.bfloat16),
            pltpu.VMEM((3, 4, 4, 2, 2, BLK, HD), jnp.bfloat16),
            pltpu.VMEM((2, 4, 4, BLK, HD), jnp.bfloat16),
            pltpu.VMEM((2 * BLK, QH * HD), jnp.bfloat16),
            pltpu.VMEM((2, PART * BLK, HD), jnp.bfloat16),
            pltpu.VMEM((2, PART * BLK, HD), jnp.bfloat16),
            pltpu.VMEM((2, QH * BLK, PART * BLK), jnp.float32),
            pltpu.VMEM((2, QH * BLK, 2 * HD), jnp.float32),
            pltpu.VMEM((2, QH * BLK, HD), jnp.float32),
            pltpu.VMEM((2, 4, BLK, HD), jnp.bfloat16),
            pltpu.VMEM((2, 3, BLK, HD), jnp.bfloat16),
            pltpu.VMEM((2, BLK, HD), jnp.bfloat16),
            pltpu.VMEM((BLK, HD), jnp.bfloat16),
            dma((4,)),
            dma((2,)), dma((2, 3)), dma((2, 2)),
            dma((2, 3, 3)), dma((2, 3, 3)),
            dma((2, 3, 3)), dma((2, 3, 3)),
            dma((2, 3, 2)), dma((2, 3, 2)),
            dma((2, 3, 4)), dma((2, 3, 4)),
            dma((2, 3)), dma((2, 3)),
            dma, dma,
            dma((6,)), dma,
            dma((3,)), dma((3,)),
            dma((3,)), dma((3,)),
            dma, dma,
            dma, dma,
        ],
        compiler_params=pltpu.CompilerParams(collective_id=0, has_side_effects=True, vmem_limit_bytes=60 * 1024 * 1024),
    )(block_list, block_count, queries, key_cache.reshape(2, BLK, HD), value_cache.reshape(2, BLK, HD))


def solution(mesh):
    placed = (P("pb", None), P(("ka", "pb"), None), P(("ka", "pb"), None), P("pb", None), P("pb"))
    return jax.shard_map(
        local_attention, mesh=mesh, in_specs=placed, out_specs=P(("pb", "ka"), None), check_vma=False
    )
```

```python
import functools
import math

import jax
import jax.numpy as jnp
from jax import lax
from jax.experimental import pallas as pl
from jax.experimental.pallas import tpu as pltpu
from jax.sharding import PartitionSpec as P

HD = 128
QH = 4
BLK = 128
LIST = 32
NV = 16
PART = 16
CHUNK = 4
MASKED = -1e30
FACTOR = math.log2(math.e) / math.sqrt(HD)


def attention_kernel(
    list_hbm, count_hbm, q_hbm, k_hbm, v_hbm, out_ref,
    list_ref, count_ref, pick_ref, told_ref, list_vm,
    k_win, v_win, vbuf, qs, kc, vc, s_ref, acc_ref, m_ref, part_out, part_in, half_out, half_in,
    in_sem, z_send, z_recv, f_send, p1_send, p1_recv, p2_send, p2_recv, f2_send, f2_recv, sib_send, sib_recv,
    vp_send, vp_recv, vh_send, vh_recv, vz_send, vz_recv, v1_send, v1_recv, v2_send, v2_recv, vs_send, vs_recv, tell_send, tell_recv,
):
    win = (k_win, v_win)
    p = lax.axis_index("pb")
    y = lax.axis_index("ka")
    z = p // 8
    x = (p // 2) % 4
    c = p % 2

    def dev(zz, xx, cc, yy):
        return (zz * 8 + xx * 2 + cc, yy)

    def remote(src, dst, ssem, rsem, device):
        return pltpu.make_async_remote_copy(
            src_ref=src, dst_ref=dst, send_sem=ssem, recv_sem=rsem,
            device_id=device, device_id_type=pl.DeviceIdType.MESH,
        )

    def have(hi):
        return z >= 2 - hi

    def needed(hi, g, xx):
        if hi == 1:
            return have(hi)
        if hi == 0:
            return have(hi) & (g >= xx)
        return g <= xx

    inputs = [
        pltpu.make_async_copy(list_hbm, list_ref, in_sem.at[0]),
        pltpu.make_async_copy(count_hbm, count_ref, in_sem.at[1]),
        pltpu.make_async_copy(q_hbm.at[pl.ds(pl.multiple_of(y * 256, 256), 256)], qs, in_sem.at[2]),
    ]
    for copy in inputs:
        copy.start()

    src = (k_hbm, v_hbm)
    g_own = z % 4
    half = 2 * y + z // 4
    z_plane = jnp.minimum(half + 1, 7)
    z_half = jnp.where(half == 7, 2, 1)

    def z_target(kv):
        xd, yd = (x, g_own) if kv == 0 else (g_own, x)
        return z_plane, xd, c, yd

    def z_source(kv, h):
        return (4 * (h % 2) + y, x, c, h // 2) if kv == 0 else (4 * (h % 2) + x, y, c, h // 2)

    def here(device):
        zz, xx, _, yy = device
        return (zz == z) & (xx == x) & (yy == y)

    barrier = pltpu.get_barrier_semaphore()
    partners = []
    always = z >= 0
    for i in range(1, 4):
        partners.append((always, (z, (x + i) % 4, c, y)))
        partners.append((always, (z, x, c, (y + i) % 4)))
    partners.append((always, (z, x, 1 - c, y)))
    partners.append((z >= 1, (jnp.maximum(z - 1, 0), x, c, y)))
    partners.append((z <= 6, (jnp.minimum(z + 1, 7), x, c, y)))
    for i in range(6):
        partners.append((z == 1, (2 + i, x, c, y)))
    partners.append((z >= 2, (1, x, c, y)))
    for kv in range(2):
        there = z_target(kv)
        partners.append((jnp.logical_not(here(there)), there))
        there = z_source(kv, jnp.maximum(z - 1, 0))
        partners.append(((z >= 1) & jnp.logical_not(here(there)), there))
        there = z_source(kv, 7)
        partners.append(((z == 7) & jnp.logical_not(here(there)), there))
    expected = jnp.int32(0)
    for live, there in partners:

        @pl.when(live)
        def _():
            pl.semaphore_signal(barrier, inc=1, device_id=dev(*there), device_id_type=pl.DeviceIdType.MESH)

        expected = expected + jnp.where(live, 1, 0)
    pl.semaphore_wait(barrier, expected)

    def z_copy(kv):
        region = win[kv].at[z_half, g_own, x, c]
        return remote(src[kv], region, z_send.at[kv], z_recv.at[kv, z_half], dev(*z_target(kv)))

    for kv in range(2):
        own = here(z_target(kv))

        @pl.when(jnp.logical_not(own))
        def _():
            z_copy(kv).start()

        @pl.when(own)
        def _():
            pltpu.make_async_copy(src[kv], win[kv].at[z_half, g_own, x, c], z_recv.at[kv, z_half]).start()

    def row(kv):
        return y if kv == 0 else x

    def col(kv):
        return x if kv == 0 else y

    def along(kv, i):
        return dev(z, (x + i) % 4, c, y) if kv == 0 else dev(z, x, c, (y + i) % 4)

    def across(kv, i):
        return dev(z, x, c, (y + i) % 4) if kv == 0 else dev(z, (x + i) % 4, c, y)

    sibling = dev(z, x, 1 - c, y)

    def p1_copy(kv, hi, i):
        region = win[kv].at[hi, row(kv), col(kv), c]
        return remote(region, region, p1_send.at[kv, hi, i - 1], p1_recv.at[kv, hi, i - 1], along(kv, i))

    def p1_live(kv, hi, i):
        if kv == 1:
            return have(hi)
        wanted = needed(hi, y, (x + i) % 4)
        return wanted | (z == 1) if hi == 2 else wanted

    def p1_got(kv, hi):
        if kv == 1:
            return have(hi)
        wanted = needed(hi, y, x)
        return wanted | (z == 1) if hi == 2 else wanted

    def p2_copy(kv, hi, i):
        region = win[kv].at[hi, row(kv), :, c]
        return remote(region, region, p2_send.at[kv, hi, i - 1], p2_recv.at[kv, hi, i - 1], across(kv, i))

    def relayed(kv, hi):
        return kv == 0 or hi == 1

    def far_copy(kv, hi, i):
        g, first = (row(kv) + 4 - i) % 4, 0 if i == 1 else 2
        region = win[kv].at[hi, g, first : first + 2, c]
        return remote(region, region, f2_send.at[kv, hi, i // 2], f2_recv.at[kv, hi, i // 2], across(kv, i))

    def p2_live(kv, hi, i):
        return needed(hi, y, x) if kv == 0 else needed(hi, x, (x + i) % 4)

    def sib_copy(kv, hi, g):
        region = win[kv].at[hi, g, :, c]
        return remote(region, region, sib_send.at[kv, hi, g], sib_recv.at[kv, hi, g], sibling)

    def vz_copy(i):
        return remote(vbuf.at[c, x, y], vbuf.at[c, x, y], vz_send.at[i], vz_recv, dev(2 + i, x, c, y))

    def v_line(first, i):
        to_x = (c == 0) == first
        return dev(z, jnp.where(to_x, (x + i) % 4, x), c, jnp.where(to_x, y, (y + i) % 4))

    def v1_copy(i):
        return remote(vbuf.at[c, x, y], vbuf.at[c, x, y], v1_send.at[i - 1], v1_recv.at[i - 1], v_line(True, i))

    def v2_copy(cc, i):
        region = vbuf.at[0, :, y] if cc == 0 else vbuf.at[1, x]
        return remote(region, region, v2_send.at[i - 1], v2_recv.at[i - 1], v_line(False, i))

    def vs_copy(cc):
        return remote(vbuf.at[cc], vbuf.at[cc], vs_send, vs_recv, sibling)

    def f_copy(kv, up):
        region = win[kv].at[1, row(kv), col(kv), c]
        there = win[kv].at[0 if up else 2, row(kv), col(kv), c]
        to = jnp.minimum(z + 1, 7) if up else jnp.maximum(z - 1, 0)
        return remote(region, there, f_send.at[kv, int(up)], z_recv.at[kv, 0 if up else 2], dev(to, x, c, y))

    def f_live(up):
        return (z >= 1) & (z <= 6) if up else z >= 1

    for copy in inputs[:2]:
        copy.wait()

    tell = remote(list_hbm, list_vm, tell_send, tell_recv, dev(1, x, c, y))

    @pl.when(z == 2)
    def _():
        tell.start()

    @pl.when(z == 1)
    def _():
        tell.wait_recv()
        told = pltpu.make_async_copy(list_vm, told_ref, in_sem.at[3])
        told.start()
        told.wait()
        entries = [told_ref[0, i] for i in range(NV)]
        slots = [4 * x + (y + i) % 4 for i in range(4)] + [4 * ((x + i) % 4) + y for i in range(4)]
        chosen = [jnp.int32(-1)] * 8
        for i in range(NV):
            rank = jnp.int32(0)
            for j in range(NV):
                if j != i:
                    rank = rank + jnp.where(entries[j] < entries[i], 1, 0)
            chosen = [jnp.where(rank == slot, entries[i], now) for slot, now in zip(slots, chosen)]
        for n in range(8):
            pick_ref[n] = chosen[n]

    for hi in (1, 0, 2):
        for kv in range(2):

            @pl.when(have(hi))
            def _():
                pltpu.make_async_copy(src[kv], win[kv].at[hi, row(kv), col(kv), c], z_recv.at[kv, hi]).wait()

            if hi == 1:
                for up in (False, True):

                    @pl.when(f_live(up))
                    def _():
                        f_copy(kv, up).start()

            for i in (1, 3, 2):

                @pl.when(p1_live(kv, hi, i))
                def _():
                    p1_copy(kv, hi, i).start()

    def p1_wait(hi):
        for kv in range(2):
            for i in (1, 3, 2):

                @pl.when(p1_got(kv, hi))
                def _():
                    region = win[kv].at[hi, row(kv), (col(kv) + 4 - i) % 4, c]
                    remote(region, region, p1_send.at[kv, hi, i - 1], p1_recv.at[kv, hi, i - 1], sibling).wait_recv()

    def p2_start(hi, when):
        for kv in range(2):
            for i in (1, 3) if relayed(kv, hi) else (1, 3, 2):

                @pl.when(p2_live(kv, hi, i) & when)
                def _():
                    p2_copy(kv, hi, i).start()

            @pl.when(needed(hi, row(kv), x) & when)
            def _():
                sib_copy(kv, hi, row(kv)).start()

    def near(hi):
        for i in (1, 3):
            for kv in range(2):
                g = (row(kv) + 4 - i) % 4

                @pl.when(needed(hi, g, x))
                def _():
                    region = win[kv].at[hi, g, :, c]
                    remote(region, region, p2_send.at[kv, hi, i - 1], p2_recv.at[kv, hi, i - 1], sibling).wait_recv()
                    if relayed(kv, hi):
                        far_copy(kv, hi, i).start()
                    sib_copy(kv, hi, g).start()

    def far(hi, kvs=(0, 1)):
        for kv in kvs:
            g = (row(kv) + 2) % 4

            @pl.when(needed(hi, g, x))
            def _():
                if relayed(kv, hi):
                    for i in (1, 3):
                        first = 0 if i == 1 else 2
                        region = win[kv].at[hi, g, first : first + 2, c]
                        remote(region, region, f2_send.at[kv, hi, i // 2], f2_recv.at[kv, hi, i // 2], sibling).wait_recv()
                else:
                    region = win[kv].at[hi, g, :, c]
                    remote(region, region, p2_send.at[kv, hi, 1], p2_recv.at[kv, hi, 1], sibling).wait_recv()
                sib_copy(kv, hi, g).start()

    def vp_copy(kv, i):
        return remote(
            part_out.at[kv, i], part_in.at[kv, i - 1], vp_send.at[kv, i - 1], vp_recv.at[kv, i - 1], across(kv, i)
        )

    def vh_copy(kv):
        return remote(half_out.at[kv], half_in, vh_send, vh_recv, sibling)

    p1_wait(1)
    p2_start(1, z >= 0)
    p1_wait(0)
    p2_start(0, z >= 0)
    p1_wait(2)

    @pl.when(z == 1)
    def _():
        for kv in range(2):

            picked = [jnp.zeros((BLK, HD), jnp.bfloat16)] * 4
            for half_name in range(2):
                for l in range(4):
                    for r in range(2):
                        block = win[kv][1 + half_name, row(kv), l, c, r]
                        name = 64 * half_name + 16 * row(kv) + 4 * l + 2 * c + r
                        picked = [jnp.where(pick_ref[4 * kv + i] == name, block, picked[i]) for i in range(4)]
            for i in range(4):
                part_out[kv, i] = picked[i]
            for i in (1, 3, 2):
                vp_copy(kv, i).start()

    p2_start(2, z >= 0)

    @pl.when(z == 1)
    def _():
        for kv in range(2):
            for i in (1, 3, 2):
                vp_copy(kv, i).wait_recv()
            half_out[kv] = (part_out[kv, 0] + part_in[kv, 0]) + (part_in[kv, 1] + part_in[kv, 2])
        vh_copy(1 - c).start()
        vh_copy(c).wait_recv()
        vbuf[c, x, y] = half_out[c] + half_in[...]
        for i in (0, 5, 1, 4, 2, 3):
            vz_copy(i).start()

    near(1)
    near(0)

    @pl.when(z >= 2)
    def _():
        vz_copy(0).wait_recv()

    @pl.when(z >= 2)
    def _():
        for i in (1, 3, 2):
            v1_copy(i).start()

    far(1)
    near(2)

    @pl.when(z >= 2)
    def _():
        for i in (1, 3, 2):
            v1_copy(i).wait_recv()
        for cc in range(2):

            @pl.when(c == cc)
            def _():
                for i in (1, 3, 2):
                    v2_copy(cc, i).start()

    far(0)
    far(2)
    def window_wait(kv):
        for hi in (1, 0, 2):
            for g in range(4):

                @pl.when(needed(hi, g, x))
                def _():
                    region = win[kv].at[hi, g, :, 1 - c]
                    remote(region, region, sib_send.at[kv, hi, g], sib_recv.at[kv, hi, g], sibling).wait_recv()

    def place(block):
        rel = jnp.clip(block - 64 * (z - 2), 0, 191)
        return rel >> 6, (rel >> 4) & 3, (rel >> 2) & 3, (rel >> 1) & 1, rel & 1

    def block_of(kv, block):
        hi, g, l, cc, r = place(block)
        return win[kv][hi, g, l, cc, r]

    delta = lax.broadcasted_iota(jnp.int32, (BLK, BLK), 1) - lax.broadcasted_iota(jnp.int32, (BLK, BLK), 0)

    ones = jnp.ones((CHUNK * BLK, HD), jnp.bfloat16)
    second_set = jnp.where(z >= 2, 0, 1)

    def keys_of(kv, q, part, n):
        if part == 1:
            return jnp.concatenate(
                [block_of(kv, list_ref[2 * y + q, PART + n * CHUNK + k]) for k in range(CHUNK)], axis=0
            )
        held = kc if kv == 0 else vc
        return held[q * second_set, n * CHUNK * BLK : (n + 1) * CHUNK * BLK, :]

    queries_of = []

    def score_chunk(q, part, n, peak):
        my_block = 8 * p + 2 * y + q
        count = count_ref[2 * y + q]
        scores = lax.dot_general(
            queries_of[q], keys_of(0, q, part, n), (((1,), (1,)), ((), ())), preferred_element_type=jnp.float32
        )
        for k in range(CHUNK):
            slot = part * PART + n * CHUNK + k
            block = list_ref[2 * y + q, slot]
            reach = jnp.where(block == my_block, 0, BLK)
            reach = jnp.where(slot < count, reach, -BLK)
            ok = delta <= reach
            tile = scores[:, k * BLK : (k + 1) * BLK].reshape(QH, BLK, BLK)
            tile = jnp.where(ok[None], tile, MASKED).reshape(QH * BLK, BLK)
            s_ref[q, :, (n * CHUNK + k) * BLK : (n * CHUNK + k + 1) * BLK] = tile
            peak = tile if peak is None else jnp.maximum(peak, tile)
        return peak

    def apply_chunk(q, part, n, top, acc):
        scores = s_ref[q, :, n * CHUNK * BLK : (n + 1) * CHUNK * BLK]
        weights = jnp.exp2((scores - top) * FACTOR).astype(jnp.bfloat16)
        values = jnp.concatenate([keys_of(1, q, part, n), ones], axis=1)
        out = jnp.dot(weights, values, preferred_element_type=jnp.float32)
        return out if acc is None else acc + out

    def stage(scored, applied, top):
        peak = acc = None
        for n in range(PART // CHUNK):
            if scored is not None:
                peak = score_chunk(*scored, n, peak)
            if applied is not None:
                acc = apply_chunk(*applied, n, top, acc)
        next_top = None if peak is None else jnp.max(peak, axis=1, keepdims=True)
        return next_top, acc

    def keep(q, top, acc):
        acc_ref[q] = acc
        m_ref[q] = jnp.broadcast_to(top, (QH * BLK, HD))

    def finish(q, top2, acc2):
        top1 = m_ref[q]
        top = jnp.maximum(top1, top2)
        f1 = jnp.exp2((top1 - top) * FACTOR)
        f2 = jnp.exp2((top2 - top) * FACTOR)
        total = f1 * acc_ref[q, :, HD:] + f2 * acc2[:, HD:]
        whole = ((f1 * acc_ref[q, :, :HD] + f2 * acc2[:, :HD]) / total).astype(jnp.bfloat16)
        for h in range(QH):
            out_ref[q * BLK : (q + 1) * BLK, h * HD : (h + 1) * HD] = whole[h * BLK : (h + 1) * BLK]

    inputs[2].wait()
    for q in range(2):
        queries_of.append(
            jnp.concatenate([qs[q * BLK : (q + 1) * BLK, h * HD : (h + 1) * HD] for h in range(QH)], axis=0)
        )

    window_wait(0)
    top_s0, _ = stage((0, 1), None, None)
    window_wait(1)

    @pl.when(z < 2)
    def _():
        def load(n, _):
            q = n // PART
            s = n % PART
            block = list_ref[2 * y + q, s]
            rows = pl.ds(pl.multiple_of(s * BLK, BLK), BLK)
            kc[q, rows, :] = block_of(0, block)
            vc[q, rows, :] = block_of(1, block)
            return 0

        lax.fori_loop(0, 2 * PART, load, 0)

    @pl.when(z >= 2)
    def _():
        for cc in range(2):

            @pl.when(c == cc)
            def _():
                for i in (1, 3, 2):
                    v2_copy(cc, i).wait_recv()
                vs_copy(cc).start()

    top_s1, acc_s0 = stage((1, 1), (0, 1), top_s0)
    keep(0, top_s0, acc_s0)

    @pl.when(z >= 2)
    def _():
        vs_copy(1 - c).wait_recv()
        kc[0] = vbuf[0].reshape(PART * BLK, HD)
        vc[0] = vbuf[1].reshape(PART * BLK, HD)

    top_v0, acc_s1 = stage((0, 0), (1, 1), top_s1)
    keep(1, top_s1, acc_s1)
    top_v1, acc_v0 = stage((1, 0), (0, 0), top_v0)
    finish(0, top_v0, acc_v0)
    _, acc_v1 = stage(None, (1, 0), top_v1)
    finish(1, top_v1, acc_v1)

    for kv in range(2):

        @pl.when(jnp.logical_not(here(z_target(kv))))
        def _():
            z_copy(kv).wait_send()

        for up in (False, True):

            @pl.when(f_live(up))
            def _():
                f_copy(kv, up).wait_send()

    for hi in range(3):
        for kv in range(2):
            for i in range(1, 4):

                @pl.when(p1_live(kv, hi, i))
                def _():
                    p1_copy(kv, hi, i).wait_send()

                if i == 2 and relayed(kv, hi):
                    continue

                @pl.when(p2_live(kv, hi, i))
                def _():
                    p2_copy(kv, hi, i).wait_send()

            for i in (1, 3) if relayed(kv, hi) else ():

                @pl.when(needed(hi, (row(kv) + 4 - i) % 4, x))
                def _():
                    far_copy(kv, hi, i).wait_send()

            for g in range(4):

                @pl.when(needed(hi, g, x))
                def _():
                    sib_copy(kv, hi, g).wait_send()

    @pl.when(z == 2)
    def _():
        tell.wait_send()

    @pl.when(z == 1)
    def _():
        for kv in range(2):
            for i in range(1, 4):
                vp_copy(kv, i).wait_send()
        vh_copy(1 - c).wait_send()
        for i in range(6):
            vz_copy(i).wait_send()

    @pl.when(z >= 2)
    def _():
        for i in range(1, 4):
            v1_copy(i).wait_send()
        for cc in range(2):

            @pl.when(c == cc)
            def _():
                for i in range(1, 4):
                    v2_copy(cc, i).wait_send()
                vs_copy(cc).wait_send()


def local_attention(queries, key_cache, value_cache, block_list, block_count):
    dma = pltpu.SemaphoreType.DMA
    rows = queries.shape[0] // 4
    return pl.pallas_call(
        attention_kernel,
        out_shape=jax.ShapeDtypeStruct((rows, QH * HD), jnp.bfloat16),
        in_specs=[
            pl.BlockSpec(memory_space=pl.ANY),
            pl.BlockSpec(memory_space=pl.ANY),
            pl.BlockSpec(memory_space=pl.ANY),
            pl.BlockSpec(memory_space=pl.ANY),
            pl.BlockSpec(memory_space=pl.ANY),
        ],
        out_specs=pl.BlockSpec(memory_space=pltpu.VMEM),
        scratch_shapes=[
            pltpu.SMEM((8, LIST), jnp.int32),
            pltpu.SMEM((8,), jnp.int32),
            pltpu.SMEM((8,), jnp.int32),
            pltpu.SMEM((8, LIST), jnp.int32),
            pltpu.VMEM((8, LIST), jnp.int32),
            pltpu.VMEM((3, 4, 4, 2, 2, BLK, HD), jnp.bfloat16),
            pltpu.VMEM((3, 4, 4, 2, 2, BLK, HD), jnp.bfloat16),
            pltpu.VMEM((2, 4, 4, BLK, HD), jnp.bfloat16),
            pltpu.VMEM((2 * BLK, QH * HD), jnp.bfloat16),
            pltpu.VMEM((2, PART * BLK, HD), jnp.bfloat16),
            pltpu.VMEM((2, PART * BLK, HD), jnp.bfloat16),
            pltpu.VMEM((2, QH * BLK, PART * BLK), jnp.float32),
            pltpu.VMEM((2, QH * BLK, 2 * HD), jnp.float32),
            pltpu.VMEM((2, QH * BLK, HD), jnp.float32),
            pltpu.VMEM((2, 4, BLK, HD), jnp.bfloat16),
            pltpu.VMEM((2, 3, BLK, HD), jnp.bfloat16),
            pltpu.VMEM((2, BLK, HD), jnp.bfloat16),
            pltpu.VMEM((BLK, HD), jnp.bfloat16),
            dma((4,)),
            dma((2,)), dma((2, 3)), dma((2, 2)),
            dma((2, 3, 3)), dma((2, 3, 3)),
            dma((2, 3, 3)), dma((2, 3, 3)),
            dma((2, 3, 2)), dma((2, 3, 2)),
            dma((2, 3, 4)), dma((2, 3, 4)),
            dma((2, 3)), dma((2, 3)),
            dma, dma,
            dma((6,)), dma,
            dma((3,)), dma((3,)),
            dma((3,)), dma((3,)),
            dma, dma,
            dma, dma,
        ],
        compiler_params=pltpu.CompilerParams(collective_id=0, has_side_effects=True, vmem_limit_bytes=60 * 1024 * 1024),
    )(block_list, block_count, queries, key_cache.reshape(2, BLK, HD), value_cache.reshape(2, BLK, HD))


def solution(mesh):
    placed = (P("pb", None), P(("ka", "pb"), None), P(("ka", "pb"), None), P("pb", None), P("pb"))
    return jax.shard_map(
        local_attention, mesh=mesh, in_specs=placed, out_specs=P(("pb", "ka"), None), check_vma=False
    )
```
